128 devices in a mesh: src: 16 (over x, y), unit: 8 (over z, core).
Axes of the slice: x: 4, y: 4, z: 4, core: 2. Of those that a mesh axis runs over, the one named last changes fastest.
Arguments:
- coeffs: float32 [384, 55], P('src'), may hold values from -6 to 6
- spectra: bfloat16 [131072, 60], P(('src', 'unit')), may hold values from -6 to 6
- epoch_weight: bfloat16 [131072], P(('src', 'unit')), may hold values from 0.25 to 4
- source_blocks: int32 [16, 24], P('src'), may hold values from 1 to 8, 64 in all within a row
- epoch_owner: int32 [131072, 1], P(('src', 'unit')), may hold values from 0 to 7; in each aligned block of 1024 rows (0 to 1023, 1024 to 2047, ...) at most 256 rows name the same one
- epoch_unit_local: int32 [131072], P(('src', 'unit')), may hold values from 0 to 255
- design: bfloat16 [2048, 3300], P('unit'), may hold values from -0.875 to 0.875
Outputs:
- new_design: float32 [2048, 3300], P('unit')
- new_coeffs: float32 [384, 55], P('src')
The draws below stay inside these ranges and needn't reach their ends.
Inputs may be any that keep to these rules, and one draw needn't show every extreme that they name: Each row of source_blocks sums to 64 and holds the value 8. `epoch_owner`: in the rows of one device no value appears more than 256 times, and one value appears exactly 256 times.
All inputs are finite; a program needn't handle non-finite values.
Results may differ from the reference program's by a relative error of at most 0.0045.
Values may be sent and summed in bfloat16 or wider, within the bound.
A program may use at most 64 MiB of HBM per device.

```python
import math
import jax
import jax.numpy as jnp
import numpy as np
from jax import lax

NCOEF = 55
NSAMP = 60
MAXB = 8
EP_DEV = 1024
UNIT_DEV = 256
CAP = 256
SRC_DEV = 24
SOURCES = 384
UNITS = 2048
EPOCHS = 131072
N_SRC = 16
N_UNIT = 8


def plant(entries, key, least, largest):
    index_at = [jax.random.randint(jax.random.fold_in(key, axis), (), 0, length) for axis, length in enumerate(entries.shape)]
    longest = entries.shape.index(max(entries.shape))
    beside = index_at[:longest] + [(index_at[longest] + 1) % entries.shape[longest]] + index_at[longest + 1:]
    return entries.at[tuple(index_at)].set(least).at[tuple(beside)].set(largest)


def level_of(own_key, dims, pieces, least, top_value):
    gain = 1.0
    for position, parts in pieces:
        draws = jax.random.uniform(jax.random.fold_in(jax.random.fold_in(own_key, 6), position), (parts,), jnp.float32, least / len(pieces), top_value / len(pieces))
        gain = gain * jnp.repeat(jnp.exp(draws), dims[position] // parts).reshape((-1,) + (1,) * (len(dims) - 1 - position))
    return gain


def profile(number_of, total, reach, skew):
    loads = [(1 << 20) // math.isqrt(grade ** skew) + 1 for grade in range(2, number_of + 1)]
    surplus, given = total - reach - (number_of - 1), [1] * (number_of - 1)
    while surplus > 0:
        free = [i for i in range(number_of - 1) if given[i] < reach]
        mass, budget = sum([loads[i] for i in free]), surplus
        for i in free:
            addition = min(reach - given[i], max(1, budget * loads[i] // mass), surplus)
            given[i] = given[i] + addition
            surplus = surplus - addition
    return np.array([reach] + given)


def ragged(rng, amount, total, most, skew):
    if amount == 2:
        one = jax.random.randint(rng, (), max(1, total - most), min(most, total - 1) + 1)
        return jnp.stack([one, total - one])
    sizes = jnp.asarray(profile(amount, total, most, skew), jnp.int32)
    pairs = (amount - 1) // 2
    donor, taker = sizes[1:1 + 2 * pairs:2], sizes[2:2 + 2 * pairs:2]
    margin = jnp.minimum(donor - 1, most - taker)
    shifted = jax.random.randint(jax.random.fold_in(rng, 1), (pairs,), 0, 1 << 20) % (margin + 1)
    sizes = sizes.at[1:1 + 2 * pairs:2].set(donor - shifted).at[2:2 + 2 * pairs:2].set(taker + shifted)
    return sizes[jax.random.permutation(jax.random.fold_in(rng, 2), amount)]


def deal_out(own_key, own, number, rows, number_of, top, bound, lean):
    ranking = jax.random.permutation(own_key, number_of)
    crowded, usual = shares(number_of, rows * top, bound, lean, True), shares(number_of, rows * top, bound, lean, False)
    places = jnp.arange(number_of)

    def named(tallies, offset_by):
        used = int((tallies > 0).sum())
        fixed = max(1, used // 4)
        shifted = fixed + (places - fixed + offset_by * (used - fixed)) % max(1, number_of - fixed)
        return jnp.zeros((number_of,), jnp.int32).at[ranking[jnp.where(places < fixed, places, shifted)]].set(jnp.asarray(tallies, jnp.int32))

    tallies = jnp.where(number % 4 == 0, named(crowded, number // 4), named(usual, number - number // 4 - 1))
    mixed = jax.random.permutation(jax.random.fold_in(own, 3), number_of)
    donor, sink = mixed[0:number_of // 2 * 2:2], mixed[1:number_of // 2 * 2:2]
    room = jnp.minimum(tallies[donor] - 1, bound - tallies[sink]) // 2
    room = jnp.where((donor == ranking[0]) | (sink == ranking[0]) | (tallies[sink] == 0), 0, jnp.maximum(room, 0))
    shifted = jax.random.randint(jax.random.fold_in(own, 4), (number_of // 2,), 0, 1 << 20) % (room + 1)
    tallies = tallies.at[donor].add(-shifted).at[sink].add(shifted)
    members = jnp.searchsorted(jnp.cumsum(tallies), jnp.arange(rows * top), side="right").astype(jnp.int32)
    table = members.reshape(top, rows).T
    table = table[jax.random.permutation(jax.random.fold_in(own, 1), rows)]
    offset_by = jax.random.randint(jax.random.fold_in(own, 2), (rows, 1), 0, top)
    return jnp.take_along_axis(table, (jnp.arange(top)[None, :] + offset_by) % top, axis=1)


def shares(number_of, total, reach, lean, full):
    loads = [(1 << 20) // math.isqrt(grade ** lean) + 1 for grade in range(1, number_of + 1)]
    largest = reach if full else min(reach, max(-(-total // number_of), total * loads[0] // sum(loads)))
    least = 1 if total - largest >= number_of - 1 else 0
    given, spare = [largest] + [least] * (number_of - 1), total - largest - least * (number_of - 1)
    while spare > 0:
        free = [i for i in range(1, number_of) if given[i] < largest] or [i for i in range(1, number_of) if given[i] < reach]
        pool, remaining = sum([loads[i] for i in free]), spare
        for i in free:
            extra = min(reach - given[i], max(1, remaining * loads[i] // pool), spare)
            given[i] = given[i] + extra
            spare = spare - extra
    return np.array(given)


def scatter_about(stream_key, dims, deviation, most, cuts=(), kind=jnp.bfloat16):
    result = deviation * jax.random.normal(stream_key, dims, jnp.float32)
    if cuts:
        result = result * level_of(stream_key, dims, cuts, -0.22, 0.18)
    return jnp.clip(result, -most, most).astype(kind)


def setup_inputs(seed: int = 0) -> dict:
    streams_of = jax.random.split(jax.random.key(seed), 8)
    coeffs = scatter_about(streams_of[0], (SOURCES, NCOEF), 1.0, 6.0, ((0, 16),), jnp.float32)
    spectra = scatter_about(streams_of[1], (EPOCHS, NSAMP), 1.0, 6.0, ((0, 128),))
    epoch_weight = jnp.clip(jnp.exp(math.log(4.0) - 2.7725887 * jax.random.uniform(streams_of[2], (EPOCHS,), jnp.float32) ** level_of(streams_of[2], (EPOCHS,), ((0, 128),), -0.2, 0.2)), 0.25, 4.0).astype(jnp.bfloat16)
    source_blocks = jax.vmap(lambda own: ragged(own, SRC_DEV, EP_DEV * N_UNIT // 128, MAXB, 2))(jax.random.split(streams_of[3], N_SRC)).reshape((N_SRC, SRC_DEV)).astype(jnp.int32)
    epoch_owner_keys = jax.random.split(jax.random.fold_in(streams_of[4], 1), EPOCHS // EP_DEV)
    epoch_owner_turns = jax.random.permutation(jax.random.fold_in(streams_of[4], 3), EPOCHS // EP_DEV)
    epoch_owner = jax.vmap(lambda own, number: deal_out(jax.random.fold_in(streams_of[4], 2), own, number, EP_DEV, N_UNIT, 1, CAP, 2))(epoch_owner_keys, epoch_owner_turns).reshape((EPOCHS, 1))
    epoch_unit_local = plant(jax.random.randint(streams_of[5], (EPOCHS,), 0, UNIT_DEV), jax.random.fold_in(streams_of[5], 1), 0, UNIT_DEV - 1).astype(jnp.int32)
    design = scatter_about(streams_of[6], (UNITS, NSAMP * NCOEF), NCOEF ** -0.5, 0.875, ((0, 8),))
    return {"coeffs": coeffs, "spectra": spectra, "epoch_weight": epoch_weight, "source_blocks": source_blocks, "epoch_owner": epoch_owner, "epoch_unit_local": epoch_unit_local, "design": design}


def reference(coeffs, spectra, epoch_weight, source_blocks, epoch_owner, epoch_unit_local, design):
    damping = 1.0
    cum = jnp.cumsum(source_blocks, axis=1)
    index = jnp.arange(EP_DEV * N_UNIT // 128, dtype=jnp.int32)
    local = jnp.sum((cum[:, None, :] <= index[None, :, None]).astype(jnp.int32), axis=2)
    block_src = (local + jnp.arange(N_SRC, dtype=jnp.int32)[:, None] * SRC_DEV).reshape(-1)
    epoch_src = jnp.repeat(block_src, 128).astype(jnp.int32)
    units_of = (epoch_owner[:, 0] * UNIT_DEV + epoch_unit_local).astype(jnp.int32)
    coef_lo = coeffs.astype(jnp.bfloat16).astype(jnp.float32)
    design3 = design.reshape(UNITS, NSAMP, NCOEF).astype(jnp.float32)
    shards = N_SRC * N_UNIT
    xs = (spectra.reshape(shards, EP_DEV, NSAMP), epoch_weight.reshape(shards, EP_DEV),
          epoch_src.reshape(shards, EP_DEV), units_of.reshape(shards, EP_DEV))

    def first(carry, x):
        spec, weight, srcs, unit = x
        c = coef_lo[srcs]
        w = weight.astype(jnp.float32)
        pred = jnp.einsum("emk,ek->em", design3[unit], c)
        q = (w[:, None] * (spec.astype(jnp.float32) - pred)).astype(jnp.bfloat16)
        q = lax.optimization_barrier(q).astype(jnp.float32)
        moment = carry[0] + jax.ops.segment_sum(q[:, :, None] * c[:, None, :], unit, UNITS)
        diag = carry[1] + jax.ops.segment_sum(w[:, None] * c * c, unit, UNITS)
        return (moment, diag), None

    init = (jnp.zeros((UNITS, NSAMP, NCOEF), jnp.float32), jnp.zeros((UNITS, NCOEF), jnp.float32))
    (moment, diag), _ = lax.scan(first, init, xs)
    new3 = design3 + moment / (diag[:, None, :] + damping)
    new_design = new3.reshape(UNITS, NSAMP * NCOEF)
    refined = new3.astype(jnp.bfloat16)
    refined = lax.optimization_barrier(refined).astype(jnp.float32)
    colsq = jnp.sum(refined * refined, axis=1)

    def second(carry, x):
        spec, weight, srcs, unit = x
        c = coef_lo[srcs]
        w = weight.astype(jnp.float32)
        local_map = refined[unit]
        pred = jnp.einsum("emk,ek->em", local_map, c)
        p = (w[:, None] * (spec.astype(jnp.float32) - pred)).astype(jnp.bfloat16)
        p = lax.optimization_barrier(p).astype(jnp.float32)
        g = jnp.einsum("emk,em->ek", local_map, p).astype(jnp.bfloat16)
        h = (w[:, None] * colsq[unit]).astype(jnp.bfloat16)
        g, h = lax.optimization_barrier((g, h))
        grad = carry[0] + jax.ops.segment_sum(g.astype(jnp.float32), srcs, SOURCES)
        hess = carry[1] + jax.ops.segment_sum(h.astype(jnp.float32), srcs, SOURCES)
        return (grad, hess), None

    init2 = (jnp.zeros((SOURCES, NCOEF), jnp.float32), jnp.zeros((SOURCES, NCOEF), jnp.float32))
    (grad, hess), _ = lax.scan(second, init2, xs)
    new_coeffs = coeffs + grad / (hess + damping)
    return new_design, new_coeffs
```

```python
import functools

import jax
import jax.numpy as jnp
from jax import lax
from jax.experimental import pallas as pl
from jax.experimental.pallas import tpu as pltpu
from jax.sharding import PartitionSpec as P

NCOEF = 55
NSAMP = 60
HALF = 64
LANES = 128
BLOCK = 128
GROUP = 16
damping = 1.0

MESH = pl.DeviceIdType.MESH
BF = jnp.bfloat16
F32 = jnp.float32


def dot(a, b):
    return jnp.dot(a, b, preferred_element_type=F32)


def dot_nt(a, b):
    return lax.dot_general(a, b, (((1,), (1,)), ((), ())), preferred_element_type=F32)


def dot_tn(a, b):
    return lax.dot_general(a, b, (((0,), (0,)), ((), ())), preferred_element_type=F32)


def iota(shape, dim):
    return lax.broadcasted_iota(jnp.int32, shape, dim)


def ones_where(mask):
    return jnp.where(mask, 1.0, 0.0).astype(BF)


def kernel(
    n_src,
    n_unit,
    nsrc,
    spec_ref,
    w_ref,
    u_ref,
    o_ref,
    cnt_ref,
    coef_ref,
    design_ref,
    gath_ref,
    nc_ref,
    dbuf,
    rank_ref,
    items_ref,
    place_ref,
    out1,
    recv1,
    acc_ref,
    xbuf,
    sbuf,
    recv2,
    sf_ref,
    cp_ref,
    fbuf,
    d2t,
    wb_ref,
    s2_ref,
    flat_ref,
    gh_ref,
    recv3,
    g1_ref,
    recv4,
    dsem,
    ssem1,
    rsem1,
    ssem2,
    rsem2,
    ssem3,
    rsem3,
    ssem4,
    rsem4,
    ssem5,
    rsem5,
):
    row = lax.axis_index("src")
    me = lax.axis_index("unit")
    epochs = spec_ref.shape[0]
    nblocks = epochs // BLOCK
    units = n_src * GROUP
    pairs = nsrc // 2
    half_slots = LANES
    width = pairs * LANES
    wide = GROUP * LANES
    rows_t = n_src * GROUP

    def unit_at(i):
        return lax.rem(me + i, n_unit)

    def row_at(i):
        return lax.rem(row + i, n_src)

    barrier = pltpu.get_barrier_semaphore()
    for i in range(1, n_unit):
        pl.semaphore_signal(barrier, inc=1, device_id={"unit": unit_at(i)}, device_id_type=MESH)
    for i in range(1, n_src):
        pl.semaphore_signal(barrier, inc=1, device_id={"src": row_at(i)}, device_id_type=MESH)

    load = pltpu.make_async_copy(
        design_ref.at[pl.ds(pl.multiple_of(row * GROUP, GROUP), GROUP)], dbuf, dsem
    )
    load.start()

    owner = o_ref[...]
    marks = jnp.concatenate(
        [jnp.where(owner == j, 1.0, 0.0) for j in range(n_unit)], axis=0
    )
    marks_lo = marks.astype(BF)
    earlier = ones_where(iota((LANES, LANES), 0) < iota((LANES, LANES), 1))
    inside = dot(marks_lo, earlier)
    totals = dot(marks_lo, jnp.ones((LANES, LANES), BF)).astype(BF)
    nrow = n_unit * nblocks
    a, b = iota((nrow, nrow), 0), iota((nrow, nrow), 1)
    before = ones_where((a // nblocks == b // nblocks) & (b < a))
    rank_ref[...] = jnp.where(marks > 0.0, inside + dot(before, totals), -1.0)

    count = jnp.broadcast_to(cnt_ref[...].astype(F32), (nblocks, nsrc)).astype(BF)
    upto = ones_where(iota((nsrc, LANES), 0) <= iota((nsrc, LANES), 1))
    cum = dot(count, upto)
    index = (me * nblocks + iota((nblocks, LANES), 0)).astype(F32)
    done = ones_where((cum <= index) & (iota((nblocks, LANES), 1) < nsrc))
    source = dot(done, jnp.ones((LANES, LANES), BF))
    meta = jnp.concatenate(
        [w_ref[...].astype(F32), u_ref[...].astype(F32), source], axis=0
    ).astype(BF)
    sub, lane = iota((NSAMP, 2 * LANES), 0), iota((NSAMP, 2 * LANES), 1)
    spread = ones_where((lane == sub) | (lane == sub + LANES + HALF))
    sub, lane = iota((3 * nblocks, 2 * LANES), 0), iota((3 * nblocks, 2 * LANES), 1)
    for block in range(nblocks):
        rows = slice(block * BLOCK, (block + 1) * BLOCK)
        pick = jnp.zeros(sub.shape, jnp.bool_)
        for field, at in enumerate((62, 63, 61)):
            here = (lane == at) | (lane == LANES + HALF + at)
            pick = pick | (here & (sub == field * nblocks + block))
        both = dot(spec_ref[rows, :], spread) + dot_tn(meta, ones_where(pick))
        both = both.astype(BF)
        items_ref[rows, :] = both[:, :LANES]
        items_ref[epochs + block * BLOCK : epochs + (block + 1) * BLOCK, :] = both[:, LANES:]

    slot = iota((LANES, LANES), 0).astype(F32)
    for i in range(n_unit):
        ranks = rank_ref[pl.ds(pl.multiple_of(unit_at(i) * nblocks, nblocks), nblocks), :]
        for block in range(nblocks):
            line = jnp.broadcast_to(ranks[block : block + 1, :], (LANES, LANES))
            at = slice(i * LANES, (i + 1) * LANES)
            place_ref[at, block * BLOCK : (block + 1) * BLOCK] = ones_where(line == slot)
            place_ref[at, epochs + block * BLOCK : epochs + (block + 1) * BLOCK] = ones_where(
                line == slot + float(half_slots)
            )
    packed = dot(place_ref[...], items_ref[...]).astype(BF)
    for i in range(n_unit):
        out1[i] = packed[i * LANES : (i + 1) * LANES]

    pl.semaphore_wait(barrier, n_unit + n_src - 2)
    sends1 = []
    for i in range(1, n_unit):
        copy = pltpu.make_async_remote_copy(
            src_ref=out1.at[i],
            dst_ref=recv1.at[i],
            send_sem=ssem1.at[i],
            recv_sem=rsem1.at[i],
            device_id={"unit": unit_at(i)},
            device_id_type=MESH,
        )
        copy.start()
        sends1.append(copy)

    coef_lo = coef_ref[...].astype(BF)
    at_row, at_src = iota((GROUP, nsrc), 0), iota((GROUP, nsrc), 1)
    k_row, k_lane = iota((NCOEF, LANES), 0), iota((NCOEF, LANES), 1)
    cp_own = jnp.zeros((GROUP, LANES), F32)
    for par in range(2):
        rows = ones_where((at_src == at_row + par * pairs) & (at_row < pairs))
        taken = dot(rows, coef_lo).astype(BF)
        cp_own = cp_own + dot(taken, ones_where(k_lane == k_row + par * HALF))
    cp_own = cp_own.astype(BF)

    load.wait()
    fbuf[...] = jnp.zeros_like(fbuf)
    own = dbuf[...].astype(F32)
    for m in range(NSAMP):
        fbuf[m * GROUP : (m + 1) * GROUP, 0:NCOEF] = own[:, m * NCOEF : (m + 1) * NCOEF]
    for u in range(GROUP):
        one = fbuf[pl.ds(u, HALF, stride=GROUP), :]
        twice = jnp.concatenate([one, one], axis=0)
        d2t[:, u * LANES : (u + 1) * LANES] = twice.T[:HALF]

    sub, lane = iota((LANES, 4 * LANES), 0), iota((LANES, 4 * LANES), 1)
    part, within = lane // LANES, lane % LANES
    data = (part < 2) & (sub == part * HALF + within % HALF) & (within % HALF < NSAMP)
    expand = ones_where(data | ((part >= 2) & (sub == (part - 2) * HALF + 61)))
    within = iota((LANES, LANES), 1) % HALF
    shift = jnp.where(iota((LANES, LANES), 1) >= HALF, float(pairs), 0.0)
    unit_row = iota((units, LANES), 0).astype(F32)
    for i in range(n_unit):
        if i == 0:
            got = out1[0]
        else:
            sends1[i - 1].wait_recv()
            got = recv1[i]
        spread4 = dot(got, expand)
        turned = got.astype(F32).T
        table = []
        for side in range(2):
            wrow = jnp.broadcast_to(turned[side * HALF + 62 : side * HALF + 63], (units, LANES))
            urow = jnp.broadcast_to(turned[side * HALF + 63 : side * HALF + 64], (units, LANES))
            table.append(jnp.where(unit_row == urow, wrow, 0.0).astype(BF))
            values = spread4[:, side * LANES : (side + 1) * LANES]
            values = jnp.where(within >= NSAMP, 1.0, values)
            which = spread4[:, (2 + side) * LANES : (3 + side) * LANES] - shift
            for t in range(pairs):
                xbuf[side * LANES : (side + 1) * LANES, t * LANES : (t + 1) * LANES] = jnp.where(
                    which == float(t), values, 0.0
                ).astype(BF)
        part_sum = dot(jnp.concatenate(table, axis=1), xbuf[...])
        if i == 0:
            acc_ref[...] = part_sum
        else:
            acc_ref[...] += part_sum

    low_lane = iota((GROUP, width), 1) % HALF == 61
    for g in range(n_src):
        rows = slice(g * GROUP, (g + 1) * GROUP)
        total = acc_ref[rows, :]
        high = total.astype(BF)
        rest = total - high.astype(F32)
        sbuf[rows, 0:width] = jnp.where(low_lane, rest, high.astype(F32)).astype(BF)
        sbuf[rows, width : width + LANES] = cp_own

    sends2 = []
    for i in range(1, n_src):
        copy = pltpu.make_async_remote_copy(
            src_ref=sbuf.at[pl.ds(pl.multiple_of(row_at(i) * GROUP, GROUP), GROUP)],
            dst_ref=recv2.at[i],
            send_sem=ssem2.at[i],
            recv_sem=rsem2.at[i],
            device_id={"src": row_at(i)},
            device_id_type=MESH,
        )
        copy.start()
        sends2.append(copy)

    for i in range(n_src):
        if i == 0:
            got = sbuf[pl.ds(pl.multiple_of(row * GROUP, GROUP), GROUP), :]
            origin = row
        else:
            sends2[i - 1].wait_recv()
            got = recv2[i]
            origin = row_at(n_src - i)
        for t in range(GROUP):
            start = pl.multiple_of((origin * GROUP + t) * GROUP, GROUP)
            if t < pairs:
                sf_ref[pl.ds(start, GROUP), :] = got[:, t * LANES : (t + 1) * LANES].astype(F32)
            else:
                sf_ref[pl.ds(start, GROUP), :] = jnp.zeros((GROUP, LANES), F32)
        cp_ref[pl.ds(pl.multiple_of(origin * GROUP, GROUP), GROUP), :] = got[:, width:]

    sub, lane = iota((LANES, 2 * LANES), 0), iota((LANES, 2 * LANES), 1) % LANES
    kind = iota((LANES, 2 * LANES), 1) // LANES
    bring = ones_where(sub == (lane // HALF) * HALF + NSAMP + kind)
    for u in range(GROUP):
        lanes = slice(u * LANES, (u + 1) * LANES)
        tile = sf_ref[pl.ds(u, rows_t, stride=GROUP), :].astype(BF)
        s2_ref[:, lanes] = tile
        weights = dot(tile, bring)
        wb_ref[0, :, lanes] = weights[:, :LANES].astype(BF)
        wb_ref[1, :, lanes] = weights[:, LANES:].astype(BF)
    cp = cp_ref[...]
    cp_wide = cp.astype(F32)
    cpt = cp_wide.T
    cpt_lo = cpt.astype(BF)
    sq = cpt * cpt
    sq_hi = sq.astype(BF)
    sq_lo = (sq - sq_hi.astype(F32)).astype(BF)
    lane = iota((HALF, wide), 1)
    first = lane % LANES < HALF
    real = lane % HALF < NSAMP

    def two_halves(x):
        return jnp.concatenate(
            [jnp.where(first, x, 0.0), jnp.where(first, 0.0, x)], axis=0
        ).astype(BF)

    def fold(x):
        y = jnp.where(first, x[:HALF], x[HALF:])
        return jnp.concatenate(
            [
                y[:, u * LANES : (u + 1) * LANES]
                + pltpu.roll(y[:, u * LANES : (u + 1) * LANES], HALF, 1)
                for u in range(GROUP)
            ],
            axis=1,
        )

    sums = s2_ref[...].astype(F32)
    weight = wb_ref[0].astype(F32) + wb_ref[1].astype(F32)
    base = d2t[...]
    resid = (sums - weight * dot(cp, two_halves(base))).astype(BF)
    moment = fold(dot(cpt_lo, resid))
    diag = fold(dot(sq_hi, wb_ref[0]) + dot(sq_lo, wb_ref[0]) + dot(sq_hi, wb_ref[1]))
    refined = jnp.where(real, base + moment / (diag + damping), 0.0).astype(BF)
    refined_wide = refined.astype(F32)
    maps = two_halves(refined_wide)
    resid = (sums - weight * dot(cp, maps)).astype(BF)
    square = refined_wide * refined_wide
    square_hi = square.astype(BF)
    square_lo = (square - square_hi.astype(F32)).astype(BF)
    firsts = ones_where(iota((LANES, LANES), 0) < HALF)
    colsq = jnp.concatenate(
        [
            dot(square_hi[:, u * LANES : (u + 1) * LANES], firsts)
            + dot(square_lo[:, u * LANES : (u + 1) * LANES], firsts)
            for u in range(GROUP)
        ],
        axis=1,
    )
    colsq_hi = colsq.astype(BF).astype(F32)
    place = lane % HALF
    curve = jnp.where((place == 60) | (place == 61), colsq_hi, 0.0)
    curve = jnp.where(place == 62, colsq - colsq_hi, curve)
    both = jnp.concatenate([maps, two_halves(curve)], axis=0)
    gh_ref[...] = dot_nt(resid, both)

    sends3 = []
    for i in range(1, n_src):
        copy = pltpu.make_async_remote_copy(
            src_ref=gh_ref.at[pl.ds(pl.multiple_of(row_at(i) * GROUP, GROUP), GROUP)],
            dst_ref=recv3.at[i],
            send_sem=ssem3.at[i],
            recv_sem=rsem3.at[i],
            device_id={"src": row_at(i)},
            device_id_type=MESH,
        )
        copy.start()
        sends3.append(copy)

    maps_wide = maps.astype(F32)
    for u in range(GROUP):
        turned = maps_wide[:, u * LANES : (u + 1) * LANES].T
        fbuf[pl.ds(u, HALF, stride=GROUP), :] = turned[:HALF]
    pieces = [fbuf[m * GROUP : (m + 1) * GROUP, 0:NCOEF] for m in range(NSAMP)]
    filler = jnp.zeros((GROUP, flat_ref.shape[1] - NSAMP * NCOEF), F32)
    flat_ref[...] = jnp.concatenate(pieces + [filler], axis=1).astype(BF)
    mine = pl.ds(pl.multiple_of(row * GROUP, GROUP), GROUP)
    keep = pltpu.make_async_copy(flat_ref, gath_ref.at[mine], dsem)
    keep.start()
    sends5 = []
    for i in range(1, n_src):
        copy = pltpu.make_async_remote_copy(
            src_ref=flat_ref,
            dst_ref=gath_ref.at[mine],
            send_sem=ssem5.at[i],
            recv_sem=rsem5.at[i],
            device_id={"src": row_at(i)},
            device_id_type=MESH,
        )
        copy.start()
        sends5.append(copy)

    total = gh_ref[pl.ds(pl.multiple_of(row * GROUP, GROUP), GROUP), :]
    for i in range(1, n_src):
        sends3[i - 1].wait_recv()
        total = total + recv3[i]
    g1_ref[...] = total
    sends4 = []
    for i in range(1, n_unit):
        copy = pltpu.make_async_remote_copy(
            src_ref=g1_ref,
            dst_ref=recv4.at[me],
            send_sem=ssem4.at[i],
            recv_sem=rsem4.at[i],
            device_id={"unit": unit_at(i)},
            device_id_type=MESH,
        )
        copy.start()
        sends4.append(copy)
    recv4[me] = total
    for copy in sends4:
        copy.wait_recv()
    total = recv4[0]
    for j in range(1, n_unit):
        total = total + recv4[j]
    step = total[:, :LANES] / (total[:, LANES:] + damping)
    other = pltpu.roll(step, HALF, 1)
    coef = coef_ref[...]
    nc_ref[0:pairs, :] = coef[0:pairs] + step[0:pairs, 0:NCOEF]
    nc_ref[pairs:nsrc, :] = coef[pairs:nsrc] + other[0:pairs, 0:NCOEF]

    keep.wait()
    for copy in sends5:
        copy.wait_recv()
    for copy in sends1 + sends2 + sends3 + sends4 + sends5:
        copy.wait_send()


def body(coeffs, spectra, epoch_weight, source_blocks, epoch_owner, epoch_unit_local, design):
    n_src = lax.axis_size("src")
    n_unit = lax.axis_size("unit")
    epochs = spectra.shape[0]
    nblocks = epochs // BLOCK
    nsrc = coeffs.shape[0]
    units, flat = design.shape
    padded = -(-flat // LANES) * LANES
    width = (nsrc // 2) * LANES
    rows_t = n_src * GROUP
    wide = GROUP * LANES
    vmem = pl.BlockSpec(memory_space=pltpu.VMEM)
    any_space = pl.BlockSpec(memory_space=pl.ANY)
    sems = pltpu.SemaphoreType.DMA
    gathered, new_coeffs = pl.pallas_call(
        functools.partial(kernel, n_src, n_unit, nsrc),
        out_shape=(
            jax.ShapeDtypeStruct((units, padded), BF),
            jax.ShapeDtypeStruct(coeffs.shape, F32),
        ),
        in_specs=[vmem] * 6 + [any_space],
        out_specs=(any_space, vmem),
        scratch_shapes=[
            pltpu.VMEM((GROUP, flat), BF),
            pltpu.VMEM((n_unit * nblocks, LANES), F32),
            pltpu.VMEM((2 * epochs, LANES), BF),
            pltpu.VMEM((n_unit * LANES, 2 * epochs), BF),
            pltpu.VMEM((n_unit, LANES, LANES), BF),
            pltpu.VMEM((n_unit, LANES, LANES), BF),
            pltpu.VMEM((units, width), F32),
            pltpu.VMEM((2 * LANES, width), BF),
            pltpu.VMEM((units, width + LANES), BF),
            pltpu.VMEM((n_src, GROUP, width + LANES), BF),
            pltpu.VMEM((rows_t * GROUP, LANES), F32),
            pltpu.VMEM((rows_t, LANES), BF),
            pltpu.VMEM((HALF * GROUP, LANES), F32),
            pltpu.VMEM((HALF, wide), F32),
            pltpu.VMEM((2, rows_t, wide), BF),
            pltpu.VMEM((rows_t, wide), BF),
            pltpu.VMEM((GROUP, padded), BF),
            pltpu.VMEM((rows_t, 2 * LANES), F32),
            pltpu.VMEM((n_src, GROUP, 2 * LANES), F32),
            pltpu.VMEM((GROUP, 2 * LANES), F32),
            pltpu.VMEM((n_unit, GROUP, 2 * LANES), F32),
            sems,
            sems((n_unit,)),
            sems((n_unit,)),
            sems((n_src,)),
            sems((n_src,)),
            sems((n_src,)),
            sems((n_src,)),
            sems((n_unit,)),
            sems((n_unit,)),
            sems((n_src,)),
            sems((n_src,)),
        ],
        compiler_params=pltpu.CompilerParams(
            collective_id=0, has_side_effects=True, vmem_limit_bytes=48 * 1024 * 1024
        ),
    )(
        spectra,
        epoch_weight.reshape(nblocks, BLOCK),
        epoch_unit_local.reshape(nblocks, BLOCK),
        epoch_owner.reshape(nblocks, BLOCK),
        source_blocks,
        coeffs,
        design,
    )
    return (gathered[:, :flat].astype(F32), new_coeffs)


def solution(mesh):
    return jax.shard_map(
        body,
        mesh=mesh,
        in_specs=(
            P("src", None),
            P(("src", "unit"), None),
            P(("src", "unit")),
            P("src", None),
            P(("src", "unit"), None),
            P(("src", "unit")),
            P("unit", None),
        ),
        out_specs=(P("unit", None), P("src", None)),
        check_vma=False,
    )
```

```python
import functools

import jax
import jax.numpy as jnp
from jax import lax
from jax.experimental import pallas as pl
from jax.experimental.pallas import tpu as pltpu
from jax.sharding import PartitionSpec as P

NCOEF = 55
NSAMP = 60
HALF = 64
LANES = 128
BLOCK = 128
GROUP = 16
damping = 1.0

MESH = pl.DeviceIdType.MESH
BF = jnp.bfloat16
F32 = jnp.float32


def dot(a, b):
    return jnp.dot(a, b, preferred_element_type=F32)


def dot_nt(a, b):
    return lax.dot_general(a, b, (((1,), (1,)), ((), ())), preferred_element_type=F32)


def dot_tn(a, b):
    return lax.dot_general(a, b, (((0,), (0,)), ((), ())), preferred_element_type=F32)


def iota(shape, dim):
    return lax.broadcasted_iota(jnp.int32, shape, dim)


def ones_where(mask):
    return jnp.where(mask, 1.0, 0.0).astype(BF)


def kernel(
    n_src,
    n_unit,
    nsrc,
    spec_ref,
    w_ref,
    u_ref,
    o_ref,
    cnt_ref,
    coef_ref,
    design_ref,
    gath_ref,
    nc_ref,
    dbuf,
    rank_ref,
    items_ref,
    place_ref,
    out1,
    recv1,
    table_ref,
    acc_ref,
    xbuf,
    sbuf,
    recv2,
    sf_ref,
    cp_ref,
    fbuf,
    d2t,
    wb_ref,
    s2_ref,
    flat_ref,
    gh_ref,
    recv3,
    g1_ref,
    recv4,
    dsem,
    ssem1,
    rsem1,
    ssem2,
    rsem2,
    ssem3,
    rsem3,
    ssem4,
    rsem4,
    ssem5,
    rsem5,
):
    row = lax.axis_index("src")
    me = lax.axis_index("unit")
    epochs = spec_ref.shape[1]
    nblocks = epochs // BLOCK
    units = n_src * GROUP
    pairs = nsrc // 2
    slots = place_ref.shape[1]
    width = pairs * LANES
    wide = GROUP * LANES
    rows_t = n_src * GROUP

    def unit_at(i):
        return lax.rem(me + i, n_unit)

    def row_at(i):
        return lax.rem(row + i, n_src)

    barrier = pltpu.get_barrier_semaphore()
    for i in range(1, n_unit):
        pl.semaphore_signal(barrier, inc=1, device_id={"unit": unit_at(i)}, device_id_type=MESH)
    for i in range(1, n_src):
        pl.semaphore_signal(barrier, inc=1, device_id={"src": row_at(i)}, device_id_type=MESH)

    load = pltpu.make_async_copy(design_ref, dbuf, dsem)
    load.start()

    owner = o_ref[...]
    marks = jnp.concatenate(
        [jnp.where(owner == j, 1.0, 0.0) for j in range(n_unit)], axis=0
    )
    marks_lo = marks.astype(BF)
    earlier = ones_where(iota((LANES, LANES), 0) < iota((LANES, LANES), 1))
    inside = dot(marks_lo, earlier)
    totals = dot(marks_lo, jnp.ones((LANES, LANES), BF)).astype(BF)
    nrow = n_unit * nblocks
    a, b = iota((nrow, nrow), 0), iota((nrow, nrow), 1)
    before = ones_where((a // nblocks == b // nblocks) & (b < a))
    rank_ref[...] = jnp.where(marks > 0.0, inside + dot(before, totals), -1.0)

    count = jnp.broadcast_to(cnt_ref[...].astype(F32), (nblocks, nsrc)).astype(BF)
    upto = ones_where(iota((nsrc, LANES), 0) <= iota((nsrc, LANES), 1))
    cum = dot(count, upto)
    index = (me * nblocks + iota((nblocks, LANES), 0)).astype(F32)
    done = ones_where((cum <= index) & (iota((nblocks, LANES), 1) < nsrc))
    source = dot(done, jnp.ones((LANES, LANES), BF))
    weights, locals_ = w_ref[...].astype(F32), u_ref[...].astype(F32)

    def one_row(x):
        return jnp.concatenate([x[b : b + 1, :] for b in range(nblocks)], axis=1)

    spare = jnp.zeros((HALF - NSAMP - 3, epochs), F32)
    items_ref[0:48, :] = spec_ref[0:48, :]
    items_ref[48:64, :] = jnp.concatenate(
        [spec_ref[48:NSAMP, :].astype(F32), one_row(weights), one_row(locals_), one_row(source), spare],
        axis=0,
    ).astype(BF)

    pl.semaphore_wait(barrier, n_unit + n_src - 2)
    slot = iota((slots, LANES), 0).astype(F32)
    sends1 = []
    for k in range(n_unit):
        i = (k + 1) % n_unit
        ranks = rank_ref[pl.ds(pl.multiple_of(unit_at(i) * nblocks, nblocks), nblocks), :]
        for block in range(nblocks):
            line = jnp.broadcast_to(ranks[block : block + 1, :], (slots, LANES))
            place_ref[i, :, block * BLOCK : (block + 1) * BLOCK] = ones_where(line == slot)
        out1[i] = dot_nt(items_ref[...], place_ref[i]).astype(BF)
        if i > 0:
            copy = pltpu.make_async_remote_copy(
                src_ref=out1.at[i],
                dst_ref=recv1.at[i],
                send_sem=ssem1.at[i],
                recv_sem=rsem1.at[i],
                device_id={"unit": unit_at(i)},
                device_id_type=MESH,
            )
            copy.start()
            sends1.append(copy)

    coef_lo = coef_ref[...].astype(BF)
    at_row, at_src = iota((GROUP, nsrc), 0), iota((GROUP, nsrc), 1)
    k_row, k_lane = iota((NCOEF, LANES), 0), iota((NCOEF, LANES), 1)
    cp_own = jnp.zeros((GROUP, LANES), F32)
    for par in range(2):
        rows = ones_where((at_src == at_row + par * pairs) & (at_row < pairs))
        taken = dot(rows, coef_lo).astype(BF)
        cp_own = cp_own + dot(taken, ones_where(k_lane == k_row + par * HALF))
    cp_own = cp_own.astype(BF)

    load.wait()
    fbuf[...] = jnp.zeros_like(fbuf)
    at_own, at_unit = iota((GROUP, units), 0), iota((GROUP, units), 1)
    own = dot_nt(ones_where(at_unit == at_own + row * GROUP), dbuf[...])
    for m in range(NSAMP):
        fbuf[m * GROUP : (m + 1) * GROUP, 0:NCOEF] = own[:, m * NCOEF : (m + 1) * NCOEF]
    for u in range(GROUP):
        one = fbuf[pl.ds(u, HALF, stride=GROUP), :]
        twice = jnp.concatenate([one, one], axis=0)
        d2t[:, u * LANES : (u + 1) * LANES] = twice.T[:HALF]

    unit_row = iota((units, slots), 0).astype(F32)
    field = iota((HALF, slots), 0)
    group = 4
    for first in range(0, n_unit, group):
        for part in range(group):
            i = first + part
            if i == 0:
                got = out1[0]
            else:
                sends1[i - 1].wait_recv()
                got = recv1[i]
            got = got.astype(F32)
            at = slice(part * slots, (part + 1) * slots)
            wrow = jnp.broadcast_to(got[60:61], (units, slots))
            urow = jnp.broadcast_to(got[61:62], (units, slots))
            table_ref[:, at] = jnp.where(unit_row == urow, wrow, 0.0).astype(BF)
            srow = jnp.broadcast_to(got[62:63], (HALF, slots))
            values = jnp.where(field < NSAMP, got, 1.0)
            for t in range(pairs):
                for par in range(2):
                    here = slice(t * LANES + par * HALF, t * LANES + par * HALF + HALF)
                    keep = srow == float(t + par * pairs)
                    xbuf[here, at] = jnp.where(keep, values, 0.0).astype(BF)
        part_sum = dot_nt(table_ref[...], xbuf[...])
        if first == 0:
            acc_ref[...] = part_sum
        else:
            acc_ref[...] += part_sum

    low_lane = iota((GROUP, width), 1) % HALF == 61
    for g in range(n_src):
        rows = slice(g * GROUP, (g + 1) * GROUP)
        total = acc_ref[rows, :]
        high = total.astype(BF)
        rest = total - high.astype(F32)
        sbuf[rows, 0:width] = jnp.where(low_lane, rest, high.astype(F32)).astype(BF)
        sbuf[rows, width : width + LANES] = cp_own

    sends2 = []
    for i in range(1, n_src):
        copy = pltpu.make_async_remote_copy(
            src_ref=sbuf.at[pl.ds(pl.multiple_of(row_at(i) * GROUP, GROUP), GROUP)],
            dst_ref=recv2.at[i],
            send_sem=ssem2.at[i],
            recv_sem=rsem2.at[i],
            device_id={"src": row_at(i)},
            device_id_type=MESH,
        )
        copy.start()
        sends2.append(copy)

    for i in range(n_src):
        if i == 0:
            got = sbuf[pl.ds(pl.multiple_of(row * GROUP, GROUP), GROUP), :]
            origin = row
        else:
            sends2[i - 1].wait_recv()
            got = recv2[i]
            origin = row_at(n_src - i)
        for t in range(GROUP):
            start = pl.multiple_of((origin * GROUP + t) * GROUP, GROUP)
            if t < pairs:
                sf_ref[pl.ds(start, GROUP), :] = got[:, t * LANES : (t + 1) * LANES].astype(F32)
            else:
                sf_ref[pl.ds(start, GROUP), :] = jnp.zeros((GROUP, LANES), F32)
        cp_ref[pl.ds(pl.multiple_of(origin * GROUP, GROUP), GROUP), :] = got[:, width:]

    sub, lane = iota((LANES, 2 * LANES), 0), iota((LANES, 2 * LANES), 1) % LANES
    kind = iota((LANES, 2 * LANES), 1) // LANES
    bring = ones_where(sub == (lane // HALF) * HALF + NSAMP + kind)
    for u in range(GROUP):
        lanes = slice(u * LANES, (u + 1) * LANES)
        tile = sf_ref[pl.ds(u, rows_t, stride=GROUP), :].astype(BF)
        s2_ref[:, lanes] = tile
        weights = dot(tile, bring)
        wb_ref[0, :, lanes] = weights[:, :LANES].astype(BF)
        wb_ref[1, :, lanes] = weights[:, LANES:].astype(BF)
    cp = cp_ref[...]
    cp_wide = cp.astype(F32)
    cpt = cp_wide.T
    cpt_lo = cpt.astype(BF)
    sq = cpt * cpt
    sq_hi = sq.astype(BF)
    sq_lo = (sq - sq_hi.astype(F32)).astype(BF)
    lane = iota((HALF, wide), 1)
    first = lane % LANES < HALF
    real = lane % HALF < NSAMP

    def two_halves(x):
        return jnp.concatenate(
            [jnp.where(first, x, 0.0), jnp.where(first, 0.0, x)], axis=0
        ).astype(BF)

    def fold(x):
        y = jnp.where(first, x[:HALF], x[HALF:])
        return jnp.concatenate(
            [
                y[:, u * LANES : (u + 1) * LANES]
                + pltpu.roll(y[:, u * LANES : (u + 1) * LANES], HALF, 1)
                for u in range(GROUP)
            ],
            axis=1,
        )

    sums = s2_ref[...].astype(F32)
    weight = wb_ref[0].astype(F32) + wb_ref[1].astype(F32)
    base = d2t[...]
    resid = (sums - weight * dot(cp, two_halves(base))).astype(BF)
    moment = fold(dot(cpt_lo, resid))
    diag = fold(dot(sq_hi, wb_ref[0]) + dot(sq_lo, wb_ref[0]) + dot(sq_hi, wb_ref[1]))
    refined = jnp.where(real, base + moment / (diag + damping), 0.0).astype(BF)
    refined_wide = refined.astype(F32)
    maps = two_halves(refined_wide)
    resid = (sums - weight * dot(cp, maps)).astype(BF)
    square = refined_wide * refined_wide
    square_hi = square.astype(BF)
    square_lo = (square - square_hi.astype(F32)).astype(BF)
    firsts = ones_where(iota((LANES, LANES), 0) < HALF)
    colsq = jnp.concatenate(
        [
            dot(square_hi[:, u * LANES : (u + 1) * LANES], firsts)
            + dot(square_lo[:, u * LANES : (u + 1) * LANES], firsts)
            for u in range(GROUP)
        ],
        axis=1,
    )
    colsq_hi = colsq.astype(BF).astype(F32)
    place = lane % HALF
    curve = jnp.where((place == 60) | (place == 61), colsq_hi, 0.0)
    curve = jnp.where(place == 62, colsq - colsq_hi, curve)
    both = jnp.concatenate([maps, two_halves(curve)], axis=0)
    gh_ref[...] = dot_nt(resid, both)

    sends3 = []
    for i in range(1, n_src):
        copy = pltpu.make_async_remote_copy(
            src_ref=gh_ref.at[pl.ds(pl.multiple_of(row_at(i) * GROUP, GROUP), GROUP)],
            dst_ref=recv3.at[i],
            send_sem=ssem3.at[i],
            recv_sem=rsem3.at[i],
            device_id={"src": row_at(i)},
            device_id_type=MESH,
        )
        copy.start()
        sends3.append(copy)

    maps_wide = maps.astype(F32)
    for u in range(GROUP):
        turned = maps_wide[:, u * LANES : (u + 1) * LANES].T
        fbuf[pl.ds(u, HALF, stride=GROUP), :] = turned[:HALF]
    pieces = [fbuf[m * GROUP : (m + 1) * GROUP, 0:NCOEF] for m in range(NSAMP)]
    filler = jnp.zeros((GROUP, flat_ref.shape[1] - NSAMP * NCOEF), F32)
    flat_ref[...] = jnp.concatenate(pieces + [filler], axis=1).astype(BF)
    mine = pl.ds(pl.multiple_of(row * GROUP, GROUP), GROUP)
    keep = pltpu.make_async_copy(flat_ref, gath_ref.at[mine], dsem)
    keep.start()
    sends5 = []
    for i in range(1, n_src):
        copy = pltpu.make_async_remote_copy(
            src_ref=flat_ref,
            dst_ref=gath_ref.at[mine],
            send_sem=ssem5.at[i],
            recv_sem=rsem5.at[i],
            device_id={"src": row_at(i)},
            device_id_type=MESH,
        )
        copy.start()
        sends5.append(copy)

    total = gh_ref[pl.ds(pl.multiple_of(row * GROUP, GROUP), GROUP), :]
    for i in range(1, n_src):
        sends3[i - 1].wait_recv()
        total = total + recv3[i]
    g1_ref[...] = total
    sends4 = []
    for i in range(1, n_unit):
        copy = pltpu.make_async_remote_copy(
            src_ref=g1_ref,
            dst_ref=recv4.at[me],
            send_sem=ssem4.at[i],
            recv_sem=rsem4.at[i],
            device_id={"unit": unit_at(i)},
            device_id_type=MESH,
        )
        copy.start()
        sends4.append(copy)
    recv4[me] = total
    for copy in sends4:
        copy.wait_recv()
    total = recv4[0]
    for j in range(1, n_unit):
        total = total + recv4[j]
    step = total[:, :LANES] / (total[:, LANES:] + damping)
    other = pltpu.roll(step, HALF, 1)
    coef = coef_ref[...]
    nc_ref[0:pairs, :] = coef[0:pairs] + step[0:pairs, 0:NCOEF]
    nc_ref[pairs:nsrc, :] = coef[pairs:nsrc] + other[0:pairs, 0:NCOEF]

    keep.wait()
    for copy in sends5:
        copy.wait_recv()
    for copy in sends1 + sends2 + sends3 + sends4 + sends5:
        copy.wait_send()


def turn_kernel(in_ref, out_ref):
    n = out_ref.shape[0]
    same = ones_where(iota((n, n), 0) == iota((n, n), 1))
    out_ref[...] = dot_nt(same, in_ref[...])


def turn(x, rows):
    units, step = x.shape[0], 2 * LANES
    return pl.pallas_call(
        turn_kernel,
        out_shape=jax.ShapeDtypeStruct((rows, units), F32),
        grid=(-(-rows // step),),
        in_specs=[pl.BlockSpec((units, step), lambda i: (0, i))],
        out_specs=pl.BlockSpec((step, units), lambda i: (i, 0)),
    )(x)


def body(coeffs, spectra, epoch_weight, source_blocks, epoch_owner, epoch_unit_local, design):
    n_src = lax.axis_size("src")
    n_unit = lax.axis_size("unit")
    epochs = spectra.shape[0]
    nblocks = epochs // BLOCK
    nsrc = coeffs.shape[0]
    units, flat = design.shape
    padded = -(-flat // LANES) * LANES
    width = (nsrc // 2) * LANES
    rows_t = n_src * GROUP
    wide = GROUP * LANES
    slots = epochs // 4
    vmem = pl.BlockSpec(memory_space=pltpu.VMEM)
    any_space = pl.BlockSpec(memory_space=pl.ANY)
    sems = pltpu.SemaphoreType.DMA
    gathered, new_coeffs = pl.pallas_call(
        functools.partial(kernel, n_src, n_unit, nsrc),
        out_shape=(
            jax.ShapeDtypeStruct((units, padded), BF),
            jax.ShapeDtypeStruct(coeffs.shape, F32),
        ),
        in_specs=[vmem] * 6 + [any_space],
        out_specs=(any_space, vmem),
        scratch_shapes=[
            pltpu.VMEM((flat, units), BF),
            pltpu.VMEM((n_unit * nblocks, LANES), F32),
            pltpu.VMEM((HALF, epochs), BF),
            pltpu.VMEM((n_unit, slots, epochs), BF),
            pltpu.VMEM((n_unit, HALF, slots), BF),
            pltpu.VMEM((n_unit, HALF, slots), BF),
            pltpu.VMEM((units, 4 * slots), BF),
            pltpu.VMEM((units, width), F32),
            pltpu.VMEM((width, 4 * slots), BF),
            pltpu.VMEM((units, width + LANES), BF),
            pltpu.VMEM((n_src, GROUP, width + LANES), BF),
            pltpu.VMEM((rows_t * GROUP, LANES), F32),
            pltpu.VMEM((rows_t, LANES), BF),
            pltpu.VMEM((HALF * GROUP, LANES), F32),
            pltpu.VMEM((HALF, wide), F32),
            pltpu.VMEM((2, rows_t, wide), BF),
            pltpu.VMEM((rows_t, wide), BF),
            pltpu.VMEM((GROUP, padded), BF),
            pltpu.VMEM((rows_t, 2 * LANES), F32),
            pltpu.VMEM((n_src, GROUP, 2 * LANES), F32),
            pltpu.VMEM((GROUP, 2 * LANES), F32),
            pltpu.VMEM((n_unit, GROUP, 2 * LANES), F32),
            sems,
            sems((n_unit,)),
            sems((n_unit,)),
            sems((n_src,)),
            sems((n_src,)),
            sems((n_src,)),
            sems((n_src,)),
            sems((n_unit,)),
            sems((n_unit,)),
            sems((n_src,)),
            sems((n_src,)),
        ],
        compiler_params=pltpu.CompilerParams(
            collective_id=0, has_side_effects=True, vmem_limit_bytes=48 * 1024 * 1024
        ),
    )(
        spectra.T,
        epoch_weight.reshape(nblocks, BLOCK),
        epoch_unit_local.reshape(nblocks, BLOCK),
        epoch_owner.reshape(nblocks, BLOCK),
        source_blocks,
        coeffs,
        design.T,
    )
    return (turn(gathered, flat).T, new_coeffs)


def solution(mesh):
    return jax.shard_map(
        body,
        mesh=mesh,
        in_specs=(
            P("src", None),
            P(("src", "unit"), None),
            P(("src", "unit")),
            P("src", None),
            P(("src", "unit"), None),
            P(("src", "unit")),
            P("unit", None),
        ),
        out_specs=(P("unit", None), P("src", None)),
        check_vma=False,
    )
```

```python
import functools
import math

import jax
import jax.numpy as jnp
from jax import lax
from jax.experimental import pallas as pl
from jax.experimental.pallas import tpu as pltpu
from jax.sharding import PartitionSpec as P

NCOEF = 55
NSAMP = 60
HALF = 64
LANES = 128
BLOCK = 128
SLOTS = 256
damping = 1.0

MESH = pl.DeviceIdType.MESH
BF = jnp.bfloat16
F32 = jnp.float32


def dot(a, b):
    return jnp.dot(a, b, preferred_element_type=F32)


def dot_nt(a, b):
    return lax.dot_general(a, b, (((1,), (1,)), ((), ())), preferred_element_type=F32)


def iota(shape, dim):
    return lax.broadcasted_iota(jnp.int32, shape, dim)


def ones_where(mask):
    return jnp.where(mask, 1.0, 0.0).astype(BF)


def split(x):
    high = x.astype(BF)
    return high, (x - high.astype(F32)).astype(BF)


def up(x, n):
    return -(-x // n) * n


def kernel(
    n_src,
    n_unit,
    nsrc,
    spec_hbm,
    w_hbm,
    u_hbm,
    o_hbm,
    cnt_hbm,
    coef_hbm,
    design_hbm,
    out_ref,
    nc_ref,
    spec_ref,
    w_ref,
    u_ref,
    o_ref,
    cnt_ref,
    coef_ref,
    dbuf,
    rank_ref,
    items_ref,
    place_ref,
    out1,
    recv1,
    cown,
    crecv,
    c_ref,
    dk_ref,
    table_ref,
    mark_ref,
    xbuf,
    sbuf,
    recv2,
    sf_ref,
    w2_ref,
    wlow_ref,
    emap,
    eflat,
    gbuf,
    gh_ref,
    csq_ref,
    recv3,
    g1_ref,
    recv4,
    lsem,
    csem,
    crsem,
    ssem1,
    rsem1,
    ssem2,
    rsem2,
    ssem3,
    rsem3,
    ssem4,
    rsem4,
    ssem5,
    ssem6,
    rsem5,
):
    row = lax.axis_index("src")
    me = lax.axis_index("unit")
    epochs = spec_ref.shape[1]
    nblocks = epochs // BLOCK
    units = 2 * LANES
    groups = n_src // 2
    samples = HALF // groups
    part_rows = samples * nsrc
    all_src = n_src * nsrc
    side = math.isqrt(n_src)
    flat = dbuf.shape[0]
    owner_rows = samples * NCOEF
    half_rows = eflat.shape[0] // 2
    my_half, my_group = row // groups, row % groups

    def unit_at(i):
        return lax.rem(me + i, n_unit)

    def row_at(i):
        return lax.rem(row + i, n_src)

    def loop(lo, hi):
        return pl.loop(lo, hi)

    barrier = pltpu.get_barrier_semaphore()

    @loop(1, n_unit)
    def _(i):
        pl.semaphore_signal(barrier, inc=1, device_id={"unit": unit_at(i)}, device_id_type=MESH)

    @loop(1, n_src)
    def _(i):
        pl.semaphore_signal(barrier, inc=1, device_id={"src": row_at(i)}, device_id_type=MESH)

    loads = [
        pltpu.make_async_copy(a, b, lsem.at[n])
        for n, (a, b) in enumerate(
            [
                (o_hbm, o_ref),
                (cnt_hbm, cnt_ref),
                (w_hbm, w_ref),
                (u_hbm, u_ref),
                (spec_hbm, spec_ref),
                (coef_hbm, coef_ref),
                (design_hbm, dbuf),
            ]
        )
    ]
    for load in loads:
        load.start()
    for load in loads[:-1]:
        load.wait()

    owner = o_ref[...]
    marks = jnp.concatenate([jnp.where(owner == j, 1.0, 0.0) for j in range(n_unit)], axis=0)
    marks_lo = marks.astype(BF)
    earlier = ones_where(iota((LANES, LANES), 0) < iota((LANES, LANES), 1))
    inside = dot(marks_lo, earlier)
    totals = dot(marks_lo, jnp.ones((LANES, LANES), BF)).astype(BF)
    nrow = n_unit * nblocks
    a, b = iota((nrow, nrow), 0), iota((nrow, nrow), 1)
    before = ones_where((a // nblocks == b // nblocks) & (b < a))
    rank_ref[...] = jnp.where(marks > 0.0, inside + dot(before, totals), -1.0)

    count = jnp.broadcast_to(cnt_ref[...].astype(F32), (nblocks, nsrc)).astype(BF)
    upto = ones_where(iota((nsrc, LANES), 0) <= iota((nsrc, LANES), 1))
    cum = dot(count, upto)
    index = (me * nblocks + iota((nblocks, LANES), 0)).astype(F32)
    done = ones_where((cum <= index) & (iota((nblocks, LANES), 1) < nsrc))
    source = dot(done, jnp.ones((LANES, LANES), BF))
    weights, locals_ = w_ref[...].astype(F32), u_ref[...].astype(F32)

    def one_row(x):
        return jnp.concatenate([x[b : b + 1, :] for b in range(nblocks)], axis=1)

    spare = jnp.zeros((HALF - NSAMP - 3, epochs), F32)
    items_ref[0:48, :] = spec_ref[0:48, :]
    items_ref[48:64, :] = jnp.concatenate(
        [
            spec_ref[48:NSAMP, :].astype(F32),
            one_row(weights),
            one_row(locals_),
            one_row(source),
            spare,
        ],
        axis=0,
    ).astype(BF)

    coef_lo = coef_ref[...].astype(BF)
    widen = ones_where(iota((NCOEF, LANES), 0) == iota((NCOEF, LANES), 1))
    deepen = ones_where(iota((cown.shape[0], nsrc), 0) == iota((cown.shape[0], nsrc), 1))
    padded = dot(deepen, dot(coef_lo, widen).astype(BF)).astype(BF)
    cown[...] = padded
    crecv[row] = padded

    pl.semaphore_wait(barrier, n_unit + n_src - 2)

    def send1(i):
        return pltpu.make_async_remote_copy(
            src_ref=out1.at[i],
            dst_ref=recv1.at[i],
            send_sem=ssem1.at[i],
            recv_sem=rsem1.at[i],
            device_id={"unit": unit_at(i)},
            device_id_type=MESH,
        )

    def send_coef(i):
        return pltpu.make_async_remote_copy(
            src_ref=cown,
            dst_ref=crecv.at[row],
            send_sem=csem.at[i],
            recv_sem=crsem.at[i],
            device_id={"src": row_at(i)},
            device_id_type=MESH,
        )

    slot = iota((SLOTS, LANES), 0).astype(F32)

    @loop(0, n_unit)
    def _(k):
        i = lax.rem(k + 1, n_unit)
        ranks = rank_ref[pl.ds(pl.multiple_of(unit_at(i) * nblocks, nblocks), nblocks), :]
        for block in range(nblocks):
            line = jnp.broadcast_to(ranks[block : block + 1, :], (SLOTS, LANES))
            place_ref[:, block * BLOCK : (block + 1) * BLOCK] = ones_where(line == slot)
        result = dot_nt(items_ref[...], place_ref[...]).astype(BF)
        out1[i] = result

        @pl.when(i > 0)
        def _():
            send1(i).start()

    @loop(1, n_src)
    def _(i):
        send_coef(i).start()

    loads[-1].wait()
    window = up(owner_rows + 15, 16)
    first_row = my_group * owner_rows
    start = jnp.minimum(first_row // 16 * 16, (flat - window) // 16 * 16)
    tail = flat // 16 * 16
    lanes_half = pl.ds(pl.multiple_of(my_half * LANES, LANES), LANES)
    shape = (samples * HALF, window)
    want = iota(shape, 0) // HALF * NCOEF + iota(shape, 0) % HALF + first_row
    real = iota(shape, 0) % HALF < NCOEF
    pick = ones_where(real & (want == iota(shape, 1) + start))
    maps = dot(pick, dbuf[pl.ds(pl.multiple_of(start, 16), window), lanes_half])
    shape = (samples * HALF, flat - tail)
    want = iota(shape, 0) // HALF * NCOEF + iota(shape, 0) % HALF + first_row
    real = iota(shape, 0) % HALF < NCOEF
    late = iota(shape, 1) + tail
    pick = ones_where(real & (want == late) & (late >= start + window))
    dk_ref[...] = maps + dot(pick, dbuf[tail:flat, lanes_half])

    unit_row = iota((units, SLOTS), 0).astype(F32)
    field = iota((HALF, SLOTS), 0)
    source_row = iota((mark_ref.shape[0], SLOTS), 0).astype(F32)
    recv1[0] = out1[0]

    @loop(0, n_unit)
    def _(i):
        @pl.when(i > 0)
        def _():
            send1(i).wait_recv()

        got = recv1[i].astype(F32)
        at = pl.ds(pl.multiple_of(i * SLOTS, SLOTS), SLOTS)
        wrow = jnp.broadcast_to(got[60:61], (units, SLOTS))
        urow = jnp.broadcast_to(got[61:62], (units, SLOTS))
        srow = got[62:63]
        table_ref[:, at] = jnp.where(unit_row == urow, wrow, 0.0).astype(BF)
        mark_ref[:, at] = ones_where(jnp.broadcast_to(srow, source_row.shape) == source_row)
        values = jnp.where(field < NSAMP, got, 0.0)
        srow = jnp.broadcast_to(srow, (samples, SLOTS))
        for s in range(0, nsrc, 2):
            one, two = srow == float(s), srow == float(s + 1)
            for g in range(groups):
                data = values[g * samples : (g + 1) * samples]
                both = jnp.concatenate([jnp.where(one, data, 0.0), jnp.where(two, data, 0.0)], axis=0)
                base = g * part_rows + s * samples
                xbuf[base : base + 2 * samples, at] = both.astype(BF)

    high, low = split(dot_nt(mark_ref[...], table_ref[...])[:nsrc])
    pair = jnp.concatenate([high.astype(F32), low.astype(F32)], axis=0).astype(BF)

    def send2(other):
        return pltpu.make_async_remote_copy(
            src_ref=sbuf.at[other],
            dst_ref=recv2.at[row],
            send_sem=ssem2.at[other],
            recv_sem=rsem2.at[row],
            device_id={"src": other},
            device_id_type=MESH,
        )

    def came2(other):
        return pltpu.make_async_remote_copy(
            src_ref=sbuf.at[other],
            dst_ref=recv2.at[other],
            send_sem=ssem2.at[other],
            recv_sem=rsem2.at[other],
            device_id={"src": other},
            device_id_type=MESH,
        )

    @loop(0, groups)
    def _(k):
        group = lax.rem(my_group + 1 + k, groups)
        x = xbuf[pl.ds(pl.multiple_of(group * part_rows, part_rows), part_rows), :]
        sums = dot_nt(x, table_ref[...]).astype(BF)
        for half in range(2):
            other = half * groups + group
            lanes = slice(half * LANES, (half + 1) * LANES)
            sbuf[other, 0:part_rows, :] = sums[:, lanes]
            sbuf[other, part_rows : part_rows + 2 * nsrc, :] = pair[:, lanes]

            @pl.when(other != row)
            def _():
                send2(other).start()

    recv2[row] = sbuf[row]

    @loop(0, n_src)
    def _(i):
        @pl.when(i > 0)
        def _():
            send_coef(i).wait_recv()

    @loop(0, n_src)
    def _(r):
        at = pl.ds(pl.multiple_of(r * nsrc, 8), nsrc)
        c_ref[at, :] = crecv[r].astype(F32)[:nsrc]

    @loop(0, n_src)
    def _(i):
        r = row_at(i)

        @pl.when(i > 0)
        def _():
            came2(r).wait_recv()

        got = recv2[r].astype(F32)
        sf_ref[pl.ds(pl.multiple_of(r * part_rows, part_rows), part_rows), :] = got[:part_rows]
        at = pl.ds(pl.multiple_of(r * nsrc, 8), nsrc)
        w2_ref[at, :] = got[part_rows : part_rows + nsrc] + got[part_rows + nsrc :]

    coef = c_ref[...]
    turned = coef.T[:HALF]
    turned_lo = turned.astype(BF)
    square_hi, square_lo = split(turned * turned)
    coef_all = coef[:, :HALF].astype(BF)
    weight_hi, weight_lo = split(w2_ref[...])
    wlow_ref[0] = weight_hi
    wlow_ref[1] = weight_lo
    diag = dot(square_hi, weight_hi) + dot(square_lo, weight_hi) + dot(square_hi, weight_lo)
    scale = 1.0 / (diag + damping)

    for m in range(samples):
        base = dk_ref[m * HALF : (m + 1) * HALF, :]
        sums = sf_ref[pl.ds(m, all_src, stride=samples), :]
        resid = (sums - w2_ref[...] * dot(coef_all, base.astype(BF))).astype(BF)
        refined = (base + dot(turned_lo, resid) * scale).astype(BF).astype(F32)
        emap[m] = refined
        dk_ref[m * NCOEF : (m + 1) * NCOEF, :] = refined[:NCOEF]
    if owner_rows < eflat.shape[0]:
        dk_ref[owner_rows : eflat.shape[0], :] = jnp.zeros((eflat.shape[0] - owner_rows, LANES), F32)
    eflat[...] = dk_ref[0 : eflat.shape[0], :].astype(BF)

    px, py = row // side, row % side

    def peer(axis, d):
        if axis == 0:
            return lax.rem(px + d, side) * side + py
        return px * side + lax.rem(py + d, side)

    def piece(half):
        return pl.ds(half * half_rows, half_rows)

    def stage1(half, d):
        return pltpu.make_async_remote_copy(
            src_ref=eflat.at[piece(half)],
            dst_ref=gbuf.at[row, piece(half)],
            send_sem=ssem5.at[half, d],
            recv_sem=rsem5.at[half, row],
            device_id={"src": peer(half, d)},
            device_id_type=MESH,
        )

    def stage2(half, q, d):
        origin = peer(half, q)
        return pltpu.make_async_remote_copy(
            src_ref=gbuf.at[origin, piece(half)],
            dst_ref=gbuf.at[origin, piece(half)],
            send_sem=ssem6.at[half, q, d],
            recv_sem=rsem5.at[half, origin],
            device_id={"src": peer(1 - half, d)},
            device_id_type=MESH,
        )

    def came5(half, origin):
        return pltpu.make_async_remote_copy(
            src_ref=gbuf.at[origin, piece(half)],
            dst_ref=gbuf.at[origin, piece(half)],
            send_sem=ssem5.at[half, 0],
            recv_sem=rsem5.at[half, origin],
            device_id={"src": row_at(1)},
            device_id_type=MESH,
        )

    gbuf[row] = eflat[...]

    @loop(1, side)
    def _(d):
        for half in range(2):
            stage1(half, d).start()

    @loop(1, side)
    def _(d):
        for half in range(2):
            stage2(half, 0, d).start()

    gh_ref[...] = jnp.zeros_like(gh_ref)
    csq_ref[...] = jnp.zeros_like(csq_ref)
    blank = jnp.zeros((HALF, LANES), F32)
    for m in range(samples):
        refined = emap[m]
        sums = sf_ref[pl.ds(m, all_src, stride=samples), :]
        resid = (sums - w2_ref[...] * dot(coef_all, refined.astype(BF))).astype(BF)
        gh_ref[...] += dot_nt(resid, jnp.concatenate([refined, blank], axis=0).astype(BF))
        csq_ref[...] += refined * refined
    curve_hi, curve_lo = split(jnp.concatenate([blank, csq_ref[...]], axis=0))
    gh_ref[...] += (
        dot_nt(wlow_ref[0], curve_hi) + dot_nt(wlow_ref[0], curve_lo) + dot_nt(wlow_ref[1], curve_hi)
    )

    def send3(i):
        return pltpu.make_async_remote_copy(
            src_ref=gh_ref.at[pl.ds(pl.multiple_of(row_at(i) * nsrc, 8), nsrc)],
            dst_ref=recv3.at[i],
            send_sem=ssem3.at[i],
            recv_sem=rsem3.at[i],
            device_id={"src": row_at(i)},
            device_id_type=MESH,
        )

    @loop(1, n_src)
    def _(i):
        send3(i).start()

    @loop(1, side)
    def _(q):
        for half in range(2):
            came5(half, peer(half, q)).wait_recv()

            @loop(1, side)
            def _(d):
                stage2(half, q, d).start()

    g1_ref[...] = gh_ref[pl.ds(pl.multiple_of(row * nsrc, 8), nsrc), :]

    @loop(1, n_src)
    def _(i):
        send3(i).wait_recv()
        g1_ref[...] += recv3[i]

    def send4(i):
        return pltpu.make_async_remote_copy(
            src_ref=g1_ref,
            dst_ref=recv4.at[me],
            send_sem=ssem4.at[i],
            recv_sem=rsem4.at[i],
            device_id={"unit": unit_at(i)},
            device_id_type=MESH,
        )

    @loop(1, n_unit)
    def _(i):
        send4(i).start()

    recv4[me] = g1_ref[...]

    @loop(1, n_unit)
    def _(i):
        send4(i).wait_recv()

    total = recv4[0]
    for j in range(1, n_unit):
        total = total + recv4[j]
    step = total / (pltpu.roll(total, HALF, 1) + damping)
    nc_ref[...] = coef_ref[...] + step[:, :NCOEF]

    def arrive(other):
        for half in range(2):
            same = (other // side == px) if half == 1 else (other % side == py)

            @pl.when(jnp.logical_not(same))
            def _():
                came5(half, other).wait_recv()

    for half in range(2):
        lanes = slice(half * LANES, (half + 1) * LANES)

        @loop(0, groups - 1)
        def _(group):
            other = half * groups + group
            arrive(other)
            at = pl.ds(pl.multiple_of(group * owner_rows, 8), owner_rows)
            out_ref[at, lanes] = gbuf[other][:owner_rows]

        other = half * groups + groups - 1
        arrive(other)
        done_rows = (groups - 1) * owner_rows
        out_ref[done_rows:flat, lanes] = gbuf[other][: flat - done_rows]

    @loop(1, n_unit)
    def _(i):
        send1(i).wait_send()
        send4(i).wait_send()

    @loop(1, n_src)
    def _(i):
        send_coef(i).wait_send()
        send2(row_at(i)).wait_send()
        send3(i).wait_send()

    @loop(1, side)
    def _(d):
        for half in range(2):
            stage1(half, d).wait_send()
            for q in range(side):
                stage2(half, q, d).wait_send()


def body(coeffs, spectra, epoch_weight, source_blocks, epoch_owner, epoch_unit_local, design):
    n_src = lax.axis_size("src")
    n_unit = lax.axis_size("unit")
    epochs = spectra.shape[0]
    nblocks = epochs // BLOCK
    nsrc = coeffs.shape[0]
    units, flat = design.shape
    groups = n_src // 2
    samples = HALF // groups
    part_rows = samples * nsrc
    message = part_rows + 2 * nsrc
    all_src = n_src * nsrc
    side = math.isqrt(n_src)
    erows = up(samples * NCOEF, 32)
    vmem = pl.BlockSpec(memory_space=pltpu.VMEM)
    hbm = pl.BlockSpec(memory_space=pltpu.HBM)
    sems = pltpu.SemaphoreType.DMA
    new_design, new_coeffs = pl.pallas_call(
        functools.partial(kernel, n_src, n_unit, nsrc),
        out_shape=(
            jax.ShapeDtypeStruct((flat, units), BF),
            jax.ShapeDtypeStruct(coeffs.shape, F32),
        ),
        in_specs=[hbm] * 7,
        out_specs=(vmem, vmem),
        scratch_shapes=[
            pltpu.VMEM((NSAMP, epochs), BF),
            pltpu.VMEM((nblocks, BLOCK), BF),
            pltpu.VMEM((nblocks, BLOCK), jnp.int32),
            pltpu.VMEM((nblocks, BLOCK), jnp.int32),
            pltpu.VMEM((1, nsrc), jnp.int32),
            pltpu.VMEM(coeffs.shape, F32),
            pltpu.VMEM((flat, units), BF),
            pltpu.VMEM((n_unit * nblocks, LANES), F32),
            pltpu.VMEM((HALF, epochs), BF),
            pltpu.VMEM((SLOTS, epochs), BF),
            pltpu.VMEM((n_unit, HALF, SLOTS), BF),
            pltpu.VMEM((n_unit, HALF, SLOTS), BF),
            pltpu.VMEM((up(nsrc, 16), LANES), BF),
            pltpu.VMEM((n_src, up(nsrc, 16), LANES), BF),
            pltpu.VMEM((all_src, LANES), F32),
            pltpu.VMEM((samples * HALF, LANES), F32),
            pltpu.VMEM((units, n_unit * SLOTS), BF),
            pltpu.VMEM((up(nsrc, 16), n_unit * SLOTS), BF),
            pltpu.VMEM((groups * part_rows, n_unit * SLOTS), BF),
            pltpu.VMEM((n_src, message, LANES), BF),
            pltpu.VMEM((n_src, message, LANES), BF),
            pltpu.VMEM((n_src * part_rows, LANES), F32),
            pltpu.VMEM((all_src, LANES), F32),
            pltpu.VMEM((2, all_src, LANES), BF),
            pltpu.VMEM((samples, HALF, LANES), F32),
            pltpu.VMEM((erows, LANES), BF),
            pltpu.VMEM((n_src, erows, LANES), BF),
            pltpu.VMEM((all_src, LANES), F32),
            pltpu.VMEM((HALF, LANES), F32),
            pltpu.VMEM((n_src, nsrc, LANES), F32),
            pltpu.VMEM((nsrc, LANES), F32),
            pltpu.VMEM((n_unit, nsrc, LANES), F32),
            sems((7,)),
            sems((n_src,)),
            sems((n_src,)),
            sems((n_unit,)),
            sems((n_unit,)),
            sems((n_src,)),
            sems((n_src,)),
            sems((n_src,)),
            sems((n_src,)),
            sems((n_unit,)),
            sems((n_unit,)),
            sems((2, side)),
            sems((2, side, side)),
            sems((2, n_src)),
        ],
        compiler_params=pltpu.CompilerParams(
            collective_id=0, has_side_effects=True, vmem_limit_bytes=56 * 1024 * 1024
        ),
    )(
        spectra.T,
        epoch_weight.reshape(nblocks, BLOCK),
        epoch_unit_local.reshape(nblocks, BLOCK),
        epoch_owner.reshape(nblocks, BLOCK),
        source_blocks,
        coeffs,
        design.T,
    )
    return (new_design.T.astype(F32), new_coeffs)


def solution(mesh):
    return jax.shard_map(
        body,
        mesh=mesh,
        in_specs=(
            P("src", None),
            P(("src", "unit"), None),
            P(("src", "unit")),
            P("src", None),
            P(("src", "unit"), None),
            P(("src", "unit")),
            P("unit", None),
        ),
        out_specs=(P("unit", None), P("src", None)),
        check_vma=False,
    )
```

```python
import functools
import math

import jax
import jax.numpy as jnp
from jax import lax
from jax.experimental import pallas as pl
from jax.experimental.pallas import tpu as pltpu
from jax.sharding import PartitionSpec as P

NCOEF = 55
NSAMP = 60
HALF = 64
LANES = 128
BLOCK = 128
SLOTS = 256
damping = 1.0

MESH = pl.DeviceIdType.MESH
BF = jnp.bfloat16
F32 = jnp.float32


def dot(a, b):
    return jnp.dot(a, b, preferred_element_type=F32)


def dot_nt(a, b):
    return lax.dot_general(a, b, (((1,), (1,)), ((), ())), preferred_element_type=F32)


def iota(shape, dim):
    return lax.broadcasted_iota(jnp.int32, shape, dim)


def ones_where(mask):
    return jnp.where(mask, 1.0, 0.0).astype(BF)


def split(x):
    high = x.astype(BF)
    return high, (x - high.astype(F32)).astype(BF)


def up(x, n):
    return -(-x // n) * n


def kernel(
    n_src,
    n_unit,
    nsrc,
    spec_hbm,
    w_hbm,
    u_hbm,
    o_hbm,
    cnt_hbm,
    coef_hbm,
    design_hbm,
    out_ref,
    nc_ref,
    spec_ref,
    w_ref,
    u_ref,
    o_ref,
    cnt_ref,
    coef_ref,
    dbuf,
    rank_ref,
    items_ref,
    place_ref,
    out1,
    recv1,
    cown,
    crecv,
    c_ref,
    dk_ref,
    table_ref,
    mark_ref,
    xbuf,
    sbuf,
    recv2,
    sf_ref,
    w2_ref,
    emap,
    eflat,
    gbuf,
    gh_ref,
    csq_ref,
    recv3,
    g1_ref,
    recv4,
    lsem,
    csem,
    crsem,
    ssem1,
    rsem1,
    ssem2,
    rsem2,
    ssem3,
    rsem3,
    ssem4,
    rsem4,
    ssem5,
    ssem6,
    rsem5,
):
    row = lax.axis_index("src")
    me = lax.axis_index("unit")
    epochs = spec_ref.shape[1]
    nblocks = epochs // BLOCK
    units = 2 * LANES
    groups = n_src // 2
    samples = HALF // groups
    part_rows = samples * nsrc
    all_src = n_src * nsrc
    head = up(nsrc, 16)
    last_samples = NSAMP - (groups - 1) * samples
    side = math.isqrt(n_src)
    flat = dbuf.shape[0]
    owner_rows = samples * NCOEF
    half_rows = eflat.shape[0] // 2
    my_half, my_group = row // groups, row % groups

    def unit_at(i):
        return lax.rem(me + i, n_unit)

    def row_at(i):
        return lax.rem(row + i, n_src)

    def loop(lo, hi):
        return pl.loop(lo, hi)

    barrier = pltpu.get_barrier_semaphore()

    @loop(1, n_unit)
    def _(i):
        pl.semaphore_signal(barrier, inc=1, device_id={"unit": unit_at(i)}, device_id_type=MESH)

    @loop(1, n_src)
    def _(i):
        pl.semaphore_signal(barrier, inc=1, device_id={"src": row_at(i)}, device_id_type=MESH)

    loads = [
        pltpu.make_async_copy(a, b, lsem.at[n])
        for n, (a, b) in enumerate(
            [
                (o_hbm, o_ref),
                (cnt_hbm, cnt_ref),
                (w_hbm, w_ref),
                (u_hbm, u_ref),
                (spec_hbm, spec_ref),
                (coef_hbm, coef_ref),
                (design_hbm, dbuf),
            ]
        )
    ]
    for load in loads:
        load.start()
    for load in loads[:-1]:
        load.wait()

    owner = o_ref[...]
    marks = jnp.concatenate([jnp.where(owner == j, 1.0, 0.0) for j in range(n_unit)], axis=0)
    marks_lo = marks.astype(BF)
    earlier = ones_where(iota((LANES, LANES), 0) < iota((LANES, LANES), 1))
    inside = dot(marks_lo, earlier)
    totals = dot(marks_lo, jnp.ones((LANES, LANES), BF)).astype(BF)
    nrow = n_unit * nblocks
    a, b = iota((nrow, nrow), 0), iota((nrow, nrow), 1)
    before = ones_where((a // nblocks == b // nblocks) & (b < a))
    rank_ref[...] = jnp.where(marks > 0.0, inside + dot(before, totals), -1.0)

    count = jnp.broadcast_to(cnt_ref[...].astype(F32), (nblocks, nsrc)).astype(BF)
    upto = ones_where(iota((nsrc, LANES), 0) <= iota((nsrc, LANES), 1))
    cum = dot(count, upto)
    index = (me * nblocks + iota((nblocks, LANES), 0)).astype(F32)
    done = ones_where((cum <= index) & (iota((nblocks, LANES), 1) < nsrc))
    source = dot(done, jnp.ones((LANES, LANES), BF))
    weights, locals_ = w_ref[...].astype(F32), u_ref[...].astype(F32)

    def one_row(x):
        return jnp.concatenate([x[b : b + 1, :] for b in range(nblocks)], axis=1)

    spare = jnp.zeros((HALF - NSAMP - 3, epochs), F32)
    items_ref[0:48, :] = spec_ref[0:48, :]
    items_ref[48:64, :] = jnp.concatenate(
        [
            spec_ref[48:NSAMP, :].astype(F32),
            one_row(weights),
            one_row(locals_),
            one_row(source),
            spare,
        ],
        axis=0,
    ).astype(BF)

    coef_lo = coef_ref[...].astype(BF)
    widen = ones_where(iota((NCOEF, LANES), 0) == iota((NCOEF, LANES), 1))
    deepen = ones_where(iota((cown.shape[0], nsrc), 0) == iota((cown.shape[0], nsrc), 1))
    padded = dot(deepen, dot(coef_lo, widen).astype(BF)).astype(BF)
    cown[...] = padded
    crecv[row] = padded

    pl.semaphore_wait(barrier, n_unit + n_src - 2)

    def send1(i):
        return pltpu.make_async_remote_copy(
            src_ref=out1.at[i],
            dst_ref=recv1.at[i],
            send_sem=ssem1.at[i],
            recv_sem=rsem1.at[i],
            device_id={"unit": unit_at(i)},
            device_id_type=MESH,
        )

    def send_coef(i):
        return pltpu.make_async_remote_copy(
            src_ref=cown,
            dst_ref=crecv.at[row],
            send_sem=csem.at[i],
            recv_sem=crsem.at[i],
            device_id={"src": row_at(i)},
            device_id_type=MESH,
        )

    slot = iota((SLOTS, LANES), 0).astype(F32)

    @loop(0, n_unit)
    def _(k):
        i = lax.rem(k + 1, n_unit)
        ranks = rank_ref[pl.ds(pl.multiple_of(unit_at(i) * nblocks, nblocks), nblocks), :]
        for block in range(nblocks):
            line = jnp.broadcast_to(ranks[block : block + 1, :], (SLOTS, LANES))
            place_ref[:, block * BLOCK : (block + 1) * BLOCK] = ones_where(line == slot)
        result = dot_nt(items_ref[...], place_ref[...]).astype(BF)
        out1[i] = result

        @pl.when(i > 0)
        def _():
            send1(i).start()

    @loop(1, n_src)
    def _(i):
        send_coef(i).start()

    loads[-1].wait()
    window = up(owner_rows + 15, 16)
    first_row = my_group * owner_rows
    start = jnp.minimum(first_row // 16 * 16, (flat - window) // 16 * 16)
    tail = flat // 16 * 16
    lanes_half = pl.ds(pl.multiple_of(my_half * LANES, LANES), LANES)
    shape = (samples * HALF, window)
    want = iota(shape, 0) // HALF * NCOEF + iota(shape, 0) % HALF + first_row
    real = iota(shape, 0) % HALF < NCOEF
    pick = ones_where(real & (want == iota(shape, 1) + start))
    maps = dot(pick, dbuf[pl.ds(pl.multiple_of(start, 16), window), lanes_half])
    shape = (samples * HALF, flat - tail)
    want = iota(shape, 0) // HALF * NCOEF + iota(shape, 0) % HALF + first_row
    real = iota(shape, 0) % HALF < NCOEF
    late = iota(shape, 1) + tail
    pick = ones_where(real & (want == late) & (late >= start + window))
    dk_ref[...] = maps + dot(pick, dbuf[tail:flat, lanes_half])

    unit_row = iota((units, SLOTS), 0).astype(F32)
    source_row = iota((mark_ref.shape[0], SLOTS), 0).astype(F32)
    recv1[0] = out1[0]

    @loop(0, n_unit)
    def _(i):
        @pl.when(i > 0)
        def _():
            send1(i).wait_recv()

        got = recv1[i].astype(F32)
        at = pl.ds(pl.multiple_of(i * SLOTS, SLOTS), SLOTS)
        wrow = jnp.broadcast_to(got[60:61], (units, SLOTS))
        urow = jnp.broadcast_to(got[61:62], (units, SLOTS))
        srow = got[62:63]
        table_ref[:, at] = jnp.where(unit_row == urow, wrow, 0.0).astype(BF)
        mark_ref[:, at] = ones_where(jnp.broadcast_to(srow, source_row.shape) == source_row)
        chosen = jnp.broadcast_to(srow, (nsrc, SLOTS)) == source_row[:nsrc]
        for m in range(0, NSAMP, 2):
            both = [
                jnp.where(chosen, jnp.broadcast_to(got[n : n + 1], (nsrc, SLOTS)), 0.0)
                for n in (m, m + 1)
            ]
            xbuf[m * nsrc : (m + 2) * nsrc, at] = jnp.concatenate(both, axis=0).astype(BF)

    weight_own = dot_nt(mark_ref[...], table_ref[...]).astype(BF)

    def copy2(other, slot, rows):
        return pltpu.make_async_remote_copy(
            src_ref=sbuf.at[other, pl.ds(0, rows)],
            dst_ref=recv2.at[slot, pl.ds(0, rows)],
            send_sem=ssem2.at[other],
            recv_sem=rsem2.at[slot],
            device_id={"src": other},
            device_id_type=MESH,
        )

    def by_group(group, act):
        @pl.when(group < groups - 1)
        def _():
            act(head + part_rows)

        @pl.when(group == groups - 1)
        def _():
            act(head + last_samples * nsrc)

    @loop(0, groups)
    def _(k):
        if side == 4:
            turn = lax.rem(k, 4)
            dy = jnp.where(turn == 0, 2, jnp.where(turn == 1, 1, jnp.where(turn == 2, 3, 0)))
            dx = jnp.where(k < 4, jnp.where(k == 1, 0, 1), jnp.where(k == 5, 1, 0))
            group = lax.rem(my_group // side + dx, 2) * side + lax.rem(my_group + dy, side)
        else:
            group = lax.rem(my_group + 1 + k, groups)
        x = xbuf[pl.ds(pl.multiple_of(group * part_rows, part_rows), part_rows), :]
        sums = dot_nt(x, table_ref[...]).astype(BF)
        for half in range(2):
            other = half * groups + group
            lanes = slice(half * LANES, (half + 1) * LANES)
            sbuf[other, 0:head, :] = weight_own[:, lanes]
            sbuf[other, head : head + part_rows, :] = sums[:, lanes]

            @pl.when(other != row)
            def _():
                by_group(group, lambda rows: copy2(other, row, rows).start())

    recv2[row] = sbuf[row]

    @loop(0, n_src)
    def _(i):
        @pl.when(i > 0)
        def _():
            send_coef(i).wait_recv()

    @loop(0, n_src)
    def _(r):
        at = pl.ds(pl.multiple_of(r * nsrc, 8), nsrc)
        c_ref[at, :] = crecv[r].astype(F32)[:nsrc]

    @loop(0, n_src)
    def _(i):
        r = row_at(i)

        @pl.when(i > 0)
        def _():
            by_group(my_group, lambda rows: copy2(r, r, rows).wait_recv())

        got = recv2[r].astype(F32)
        for m in range(samples):
            at = pl.ds(pl.multiple_of(m * all_src + r * nsrc, 8), nsrc)
            sf_ref[at, :] = got[head + m * nsrc : head + (m + 1) * nsrc]
        w2_ref[pl.ds(pl.multiple_of(r * nsrc, 8), nsrc), :] = got[:nsrc]

    coef = c_ref[...]
    turned = coef.T[:HALF]
    turned_lo = turned.astype(BF)
    square_hi, square_lo = split(turned * turned)
    coef_all = coef[:, :HALF].astype(BF)
    weight_lo = w2_ref[...].astype(BF)
    diag = dot(square_hi, weight_lo) + dot(square_lo, weight_lo)
    scale = 1.0 / (diag + damping)

    def by_samples(act):
        for m in range(last_samples):
            act(m)

        @pl.when(my_group < groups - 1)
        def _():
            for m in range(last_samples, samples):
                act(m)

    def refine(m):
        base = dk_ref[m * HALF : (m + 1) * HALF, :]
        sums = sf_ref[m * all_src : (m + 1) * all_src, :]
        resid = (sums - w2_ref[...] * dot(coef_all, base.astype(BF))).astype(BF)
        refined = (base + dot(turned_lo, resid) * scale).astype(BF).astype(F32)
        emap[m] = refined
        dk_ref[m * NCOEF : (m + 1) * NCOEF, :] = refined[:NCOEF]

    by_samples(refine)
    if owner_rows < eflat.shape[0]:
        dk_ref[owner_rows : eflat.shape[0], :] = jnp.zeros((eflat.shape[0] - owner_rows, LANES), F32)
    eflat[...] = dk_ref[0 : eflat.shape[0], :].astype(BF)

    px, py = row // side, row % side

    def peer(axis, d):
        if axis == 0:
            return lax.rem(px + d, side) * side + py
        return px * side + lax.rem(py + d, side)

    def piece(half):
        return pl.ds(half * half_rows, half_rows)

    def stage1(half, d):
        return pltpu.make_async_remote_copy(
            src_ref=eflat.at[piece(half)],
            dst_ref=gbuf.at[row, piece(half)],
            send_sem=ssem5.at[half, d],
            recv_sem=rsem5.at[half, row],
            device_id={"src": peer(half, d)},
            device_id_type=MESH,
        )

    def stage2(half, q, d):
        origin = peer(half, q)
        return pltpu.make_async_remote_copy(
            src_ref=gbuf.at[origin, piece(half)],
            dst_ref=gbuf.at[origin, piece(half)],
            send_sem=ssem6.at[half, q, d],
            recv_sem=rsem5.at[half, origin],
            device_id={"src": peer(1 - half, d)},
            device_id_type=MESH,
        )

    def came5(half, origin):
        return pltpu.make_async_remote_copy(
            src_ref=gbuf.at[origin, piece(half)],
            dst_ref=gbuf.at[origin, piece(half)],
            send_sem=ssem5.at[half, 0],
            recv_sem=rsem5.at[half, origin],
            device_id={"src": row_at(1)},
            device_id_type=MESH,
        )

    def whole(half, origin):
        if half == 0 or last_samples * NCOEF > half_rows:
            return origin >= 0
        return origin % groups != groups - 1

    gbuf[row] = eflat[...]

    @loop(1, side)
    def _(d):
        for half in range(2):

            @pl.when(whole(half, row))
            def _():
                stage1(half, d).start()

    @loop(1, side)
    def _(d):
        for half in range(2):

            @pl.when(whole(half, row))
            def _():
                stage2(half, 0, d).start()

    gh_ref[...] = jnp.zeros_like(gh_ref)
    csq_ref[...] = jnp.zeros_like(csq_ref)
    blank = jnp.zeros((HALF, LANES), F32)

    def terms(m):
        refined = emap[m]
        sums = sf_ref[m * all_src : (m + 1) * all_src, :]
        resid = (sums - w2_ref[...] * dot(coef_all, refined.astype(BF))).astype(BF)
        gh_ref[...] += dot_nt(resid, jnp.concatenate([refined, blank], axis=0).astype(BF))
        csq_ref[...] += refined * refined

    by_samples(terms)
    curve_hi, curve_lo = split(jnp.concatenate([blank, csq_ref[...]], axis=0))
    weight_lo = w2_ref[...].astype(BF)
    gh_ref[...] += dot_nt(weight_lo, curve_hi) + dot_nt(weight_lo, curve_lo)

    def send3(i):
        return pltpu.make_async_remote_copy(
            src_ref=gh_ref.at[pl.ds(pl.multiple_of(row_at(i) * nsrc, 8), nsrc)],
            dst_ref=recv3.at[i],
            send_sem=ssem3.at[i],
            recv_sem=rsem3.at[i],
            device_id={"src": row_at(i)},
            device_id_type=MESH,
        )

    @loop(1, n_src)
    def _(i):
        send3(i).start()

    @loop(1, side)
    def _(q):
        for half in range(2):

            @pl.when(whole(half, peer(half, q)))
            def _():
                came5(half, peer(half, q)).wait_recv()

                @loop(1, side)
                def _(d):
                    stage2(half, q, d).start()

    g1_ref[...] = gh_ref[pl.ds(pl.multiple_of(row * nsrc, 8), nsrc), :]

    @loop(1, n_src)
    def _(i):
        send3(i).wait_recv()
        g1_ref[...] += recv3[i]

    def send4(i):
        return pltpu.make_async_remote_copy(
            src_ref=g1_ref,
            dst_ref=recv4.at[me],
            send_sem=ssem4.at[i],
            recv_sem=rsem4.at[i],
            device_id={"unit": unit_at(i)},
            device_id_type=MESH,
        )

    @loop(1, n_unit)
    def _(i):
        send4(i).start()

    recv4[me] = g1_ref[...]

    @loop(1, n_unit)
    def _(i):
        send4(i).wait_recv()

    total = recv4[0]
    for j in range(1, n_unit):
        total = total + recv4[j]
    step = total / (pltpu.roll(total, HALF, 1) + damping)
    nc_ref[...] = coef_ref[...] + step[:, :NCOEF]

    def arrive(other):
        for half in range(2):
            same = (other // side == px) if half == 1 else (other % side == py)

            @pl.when(jnp.logical_not(same) & whole(half, other))
            def _():
                came5(half, other).wait_recv()

    for half in range(2):
        lanes = slice(half * LANES, (half + 1) * LANES)

        @loop(0, groups - 1)
        def _(group):
            other = half * groups + group
            arrive(other)
            at = pl.ds(pl.multiple_of(group * owner_rows, 8), owner_rows)
            out_ref[at, lanes] = gbuf[other][:owner_rows]

        other = half * groups + groups - 1
        arrive(other)
        done_rows = (groups - 1) * owner_rows
        out_ref[done_rows:flat, lanes] = gbuf[other][: flat - done_rows]

    @loop(1, n_unit)
    def _(i):
        send1(i).wait_send()
        send4(i).wait_send()

    @loop(1, n_src)
    def _(i):
        send_coef(i).wait_send()
        send3(i).wait_send()
        other = row_at(i)
        by_group(other % groups, lambda rows: copy2(other, row, rows).wait_send())

    @loop(1, side)
    def _(d):
        for half in range(2):

            @pl.when(whole(half, row))
            def _():
                stage1(half, d).wait_send()

            for q in range(side):

                @pl.when(whole(half, peer(half, q)))
                def _():
                    stage2(half, q, d).wait_send()


def body(coeffs, spectra, epoch_weight, source_blocks, epoch_owner, epoch_unit_local, design):
    n_src = lax.axis_size("src")
    n_unit = lax.axis_size("unit")
    epochs = spectra.shape[0]
    nblocks = epochs // BLOCK
    nsrc = coeffs.shape[0]
    units, flat = design.shape
    groups = n_src // 2
    samples = HALF // groups
    part_rows = samples * nsrc
    message = part_rows + up(nsrc, 16)
    all_src = n_src * nsrc
    side = math.isqrt(n_src)
    erows = up(samples * NCOEF, 32)
    vmem = pl.BlockSpec(memory_space=pltpu.VMEM)
    hbm = pl.BlockSpec(memory_space=pltpu.HBM)
    sems = pltpu.SemaphoreType.DMA
    new_design, new_coeffs = pl.pallas_call(
        functools.partial(kernel, n_src, n_unit, nsrc),
        out_shape=(
            jax.ShapeDtypeStruct((flat, units), BF),
            jax.ShapeDtypeStruct(coeffs.shape, F32),
        ),
        in_specs=[hbm] * 7,
        out_specs=(vmem, vmem),
        scratch_shapes=[
            pltpu.VMEM((NSAMP, epochs), BF),
            pltpu.VMEM((nblocks, BLOCK), BF),
            pltpu.VMEM((nblocks, BLOCK), jnp.int32),
            pltpu.VMEM((nblocks, BLOCK), jnp.int32),
            pltpu.VMEM((1, nsrc), jnp.int32),
            pltpu.VMEM(coeffs.shape, F32),
            pltpu.VMEM((flat, units), BF),
            pltpu.VMEM((n_unit * nblocks, LANES), F32),
            pltpu.VMEM((HALF, epochs), BF),
            pltpu.VMEM((SLOTS, epochs), BF),
            pltpu.VMEM((n_unit, HALF, SLOTS), BF),
            pltpu.VMEM((n_unit, HALF, SLOTS), BF),
            pltpu.VMEM((up(nsrc, 16), LANES), BF),
            pltpu.VMEM((n_src, up(nsrc, 16), LANES), BF),
            pltpu.VMEM((all_src, LANES), F32),
            pltpu.VMEM((samples * HALF, LANES), F32),
            pltpu.VMEM((units, n_unit * SLOTS), BF),
            pltpu.VMEM((up(nsrc, 16), n_unit * SLOTS), BF),
            pltpu.VMEM((groups * part_rows, n_unit * SLOTS), BF),
            pltpu.VMEM((n_src, message, LANES), BF),
            pltpu.VMEM((n_src, message, LANES), BF),
            pltpu.VMEM((n_src * part_rows, LANES), F32),
            pltpu.VMEM((all_src, LANES), F32),
            pltpu.VMEM((samples, HALF, LANES), F32),
            pltpu.VMEM((erows, LANES), BF),
            pltpu.VMEM((n_src, erows, LANES), BF),
            pltpu.VMEM((all_src, LANES), F32),
            pltpu.VMEM((HALF, LANES), F32),
            pltpu.VMEM((n_src, nsrc, LANES), F32),
            pltpu.VMEM((nsrc, LANES), F32),
            pltpu.VMEM((n_unit, nsrc, LANES), F32),
            sems((7,)),
            sems((n_src,)),
            sems((n_src,)),
            sems((n_unit,)),
            sems((n_unit,)),
            sems((n_src,)),
            sems((n_src,)),
            sems((n_src,)),
            sems((n_src,)),
            sems((n_unit,)),
            sems((n_unit,)),
            sems((2, side)),
            sems((2, side, side)),
            sems((2, n_src)),
        ],
        compiler_params=pltpu.CompilerParams(
            collective_id=0, has_side_effects=True, vmem_limit_bytes=44 * 1024 * 1024
        ),
    )(
        *[
            pltpu.with_memory_space_constraint(x, pltpu.HBM)
            for x in (
                spectra.T,
                epoch_weight.reshape(nblocks, BLOCK),
                epoch_unit_local.reshape(nblocks, BLOCK),
                epoch_owner.reshape(nblocks, BLOCK),
                source_blocks,
                coeffs,
                design.T,
            )
        ]
    )
    return (new_design.T.astype(F32), new_coeffs)


def solution(mesh):
    return jax.shard_map(
        body,
        mesh=mesh,
        in_specs=(
            P("src", None),
            P(("src", "unit"), None),
            P(("src", "unit")),
            P("src", None),
            P(("src", "unit"), None),
            P(("src", "unit")),
            P("unit", None),
        ),
        out_specs=(P("unit", None), P("src", None)),
        check_vma=False,
    )
```

```python
import functools
import math

import jax
import jax.numpy as jnp
from jax import lax
from jax.experimental import pallas as pl
from jax.experimental.pallas import tpu as pltpu
from jax.sharding import PartitionSpec as P

NCOEF = 55
NSAMP = 60
HALF = 64
LANES = 128
BLOCK = 128
SLOTS = 256
damping = 1.0

MESH = pl.DeviceIdType.MESH
BF = jnp.bfloat16
F32 = jnp.float32


def dot(a, b):
    return jnp.dot(a, b, preferred_element_type=F32)


def dot_nt(a, b):
    return lax.dot_general(a, b, (((1,), (1,)), ((), ())), preferred_element_type=F32)


def iota(shape, dim):
    return lax.broadcasted_iota(jnp.int32, shape, dim)


def ones_where(mask):
    return jnp.where(mask, 1.0, 0.0).astype(BF)


def split(x):
    high = x.astype(BF)
    return high, (x - high.astype(F32)).astype(BF)


def up(x, n):
    return -(-x // n) * n


def kernel(
    n_src,
    n_unit,
    nsrc,
    spec_hbm,
    w_hbm,
    u_hbm,
    o_hbm,
    cnt_hbm,
    coef_hbm,
    design_hbm,
    out_ref,
    nc_ref,
    spec_ref,
    w_ref,
    u_ref,
    o_ref,
    cnt_ref,
    coef_ref,
    dbuf,
    rank_ref,
    items_ref,
    place_ref,
    out1,
    recv1,
    cown,
    crecv,
    c_ref,
    dk_ref,
    table_ref,
    mark_ref,
    got_ref,
    xbuf,
    sbuf,
    recv2,
    sf_ref,
    w2_ref,
    emap,
    eflat,
    gbuf,
    gh_ref,
    csq_ref,
    recv3,
    g1_ref,
    recv4,
    lsem,
    csem,
    crsem,
    ssem1,
    rsem1,
    ssem2,
    rsem2,
    ssem3,
    rsem3,
    ssem4,
    rsem4,
    ssem5,
    rsem5,
):
    row = lax.axis_index("src")
    me = lax.axis_index("unit")
    epochs = spec_ref.shape[1]
    nblocks = epochs // BLOCK
    units = 2 * LANES
    groups = n_src // 2
    samples = HALF // groups
    part_rows = samples * nsrc
    all_src = n_src * nsrc
    head = up(nsrc, 16)
    last_samples = NSAMP - (groups - 1) * samples
    side = math.isqrt(n_src)
    flat = dbuf.shape[0]
    owner_rows = samples * NCOEF
    half_rows = eflat.shape[0] // 2
    my_half, my_group = row // groups, row % groups

    def unit_at(i):
        return lax.rem(me + i, n_unit)

    def row_at(i):
        return lax.rem(row + i, n_src)

    def loop(lo, hi):
        return pl.loop(lo, hi)

    barrier = pltpu.get_barrier_semaphore()

    @loop(1, n_unit)
    def _(i):
        pl.semaphore_signal(barrier, inc=1, device_id={"unit": unit_at(i)}, device_id_type=MESH)

    @loop(1, n_src)
    def _(i):
        pl.semaphore_signal(barrier, inc=1, device_id={"src": row_at(i)}, device_id_type=MESH)

    loads = [
        pltpu.make_async_copy(a, b, lsem.at[n])
        for n, (a, b) in enumerate(
            [
                (o_hbm, o_ref),
                (cnt_hbm, cnt_ref),
                (w_hbm, w_ref),
                (u_hbm, u_ref),
                (spec_hbm, spec_ref),
                (coef_hbm, coef_ref),
                (design_hbm, dbuf),
            ]
        )
    ]
    for load in loads:
        load.start()
    for load in loads[:-1]:
        load.wait()

    owner = o_ref[...]
    marks = jnp.concatenate([jnp.where(owner == j, 1.0, 0.0) for j in range(n_unit)], axis=0)
    marks_lo = marks.astype(BF)
    earlier = ones_where(iota((LANES, LANES), 0) < iota((LANES, LANES), 1))
    inside = dot(marks_lo, earlier)
    totals = dot(marks_lo, jnp.ones((LANES, LANES), BF)).astype(BF)
    nrow = n_unit * nblocks
    a, b = iota((nrow, nrow), 0), iota((nrow, nrow), 1)
    before = ones_where((a // nblocks == b // nblocks) & (b < a))
    rank_ref[...] = jnp.where(marks > 0.0, inside + dot(before, totals), -1.0)

    count = jnp.broadcast_to(cnt_ref[...].astype(F32), (nblocks, nsrc)).astype(BF)
    upto = ones_where(iota((nsrc, LANES), 0) <= iota((nsrc, LANES), 1))
    cum = dot(count, upto)
    index = (me * nblocks + iota((nblocks, LANES), 0)).astype(F32)
    done = ones_where((cum <= index) & (iota((nblocks, LANES), 1) < nsrc))
    source = dot(done, jnp.ones((LANES, LANES), BF))
    weights, locals_ = w_ref[...].astype(F32), u_ref[...].astype(F32)

    def one_row(x):
        return jnp.concatenate([x[b : b + 1, :] for b in range(nblocks)], axis=1)

    spare = jnp.zeros((HALF - NSAMP - 3, epochs), F32)
    items_ref[0:48, :] = spec_ref[0:48, :]
    items_ref[48:64, :] = jnp.concatenate(
        [
            spec_ref[48:NSAMP, :].astype(F32),
            one_row(weights),
            one_row(locals_),
            one_row(source),
            spare,
        ],
        axis=0,
    ).astype(BF)

    coef_lo = coef_ref[...].astype(BF)
    widen = ones_where(iota((NCOEF, LANES), 0) == iota((NCOEF, LANES), 1))
    deepen = ones_where(iota((cown.shape[0], nsrc), 0) == iota((cown.shape[0], nsrc), 1))
    padded = dot(deepen, dot(coef_lo, widen).astype(BF)).astype(BF)
    cown[...] = padded
    crecv[row] = padded

    pl.semaphore_wait(barrier, n_unit + n_src - 2)

    def send1(i):
        return pltpu.make_async_remote_copy(
            src_ref=out1.at[i],
            dst_ref=recv1.at[i],
            send_sem=ssem1.at[i],
            recv_sem=rsem1.at[i],
            device_id={"unit": unit_at(i)},
            device_id_type=MESH,
        )

    def send_coef(i):
        return pltpu.make_async_remote_copy(
            src_ref=cown,
            dst_ref=crecv.at[row],
            send_sem=csem.at[i],
            recv_sem=crsem.at[i],
            device_id={"src": row_at(i)},
            device_id_type=MESH,
        )

    slot = iota((SLOTS, LANES), 0).astype(F32).astype(BF)
    one, zero = jnp.ones((), BF), jnp.zeros((), BF)

    @loop(0, n_unit)
    def _(k):
        i = lax.rem(k + 1, n_unit)
        ranks = rank_ref[pl.ds(pl.multiple_of(unit_at(i) * nblocks, nblocks), nblocks), :]
        for block in range(nblocks):
            line = jnp.broadcast_to(ranks[block : block + 1, :], (SLOTS, LANES)).astype(BF)
            place_ref[:, block * BLOCK : (block + 1) * BLOCK] = jnp.where(line == slot, one, zero)
        result = dot_nt(items_ref[...], place_ref[...]).astype(BF)
        out1[i] = result

        @pl.when(i > 0)
        def _():
            send1(i).start()

    @loop(1, n_src)
    def _(i):
        send_coef(i).start()

    loads[-1].wait()
    window = up(owner_rows + 15, 16)
    first_row = my_group * owner_rows
    start = jnp.minimum(first_row // 16 * 16, (flat - window) // 16 * 16)
    tail = flat // 16 * 16
    lanes_half = pl.ds(pl.multiple_of(my_half * LANES, LANES), LANES)
    shape = (samples * HALF, window)
    want = iota(shape, 0) // HALF * NCOEF + iota(shape, 0) % HALF + first_row
    real = iota(shape, 0) % HALF < NCOEF
    pick = ones_where(real & (want == iota(shape, 1) + start))
    maps = dot(pick, dbuf[pl.ds(pl.multiple_of(start, 16), window), lanes_half])
    shape = (samples * HALF, flat - tail)
    want = iota(shape, 0) // HALF * NCOEF + iota(shape, 0) % HALF + first_row
    real = iota(shape, 0) % HALF < NCOEF
    late = iota(shape, 1) + tail
    pick = ones_where(real & (want == late) & (late >= start + window))
    dk_ref[...] = maps + dot(pick, dbuf[tail:flat, lanes_half])

    unit_row = iota((units, SLOTS), 0).astype(F32)
    source_row = iota((mark_ref.shape[0], SLOTS), 0).astype(F32)
    recv1[0] = out1[0]

    @loop(0, n_unit)
    def _(i):
        @pl.when(i > 0)
        def _():
            send1(i).wait_recv()

        got = recv1[i].astype(F32)
        at = pl.ds(pl.multiple_of(i * SLOTS, SLOTS), SLOTS)
        wrow = jnp.broadcast_to(got[60:61], (units, SLOTS))
        urow = jnp.broadcast_to(got[61:62], (units, SLOTS))
        srow = got[62:63]
        table_ref[at, :] = jnp.where(unit_row == urow, wrow, 0.0).T.astype(BF)
        chosen = jnp.broadcast_to(srow, source_row.shape) == source_row
        mark_ref[:, at] = jnp.where(chosen, 1.0, 0.0)
        got_ref[:, at] = got

    weight_own = dot(mark_ref[...].astype(BF), table_ref[...]).astype(BF)

    def copy2(other, slot, rows):
        return pltpu.make_async_remote_copy(
            src_ref=sbuf.at[other, pl.ds(0, rows)],
            dst_ref=recv2.at[slot, pl.ds(0, rows)],
            send_sem=ssem2.at[other],
            recv_sem=rsem2.at[slot],
            device_id={"src": other},
            device_id_type=MESH,
        )

    def by_group(group, act):
        @pl.when(group < groups - 1)
        def _():
            act(head + part_rows)

        @pl.when(group == groups - 1)
        def _():
            act(head + last_samples * nsrc)

    @loop(0, groups)
    def _(k):
        if side == 4:
            turn = lax.rem(k, 4)
            dy = jnp.where(turn == 0, 2, jnp.where(turn == 1, 1, jnp.where(turn == 2, 3, 0)))
            dx = jnp.where(k < 4, jnp.where(k == 1, 0, 1), jnp.where(k == 5, 1, 0))
            group = lax.rem(my_group // side + dx, 2) * side + lax.rem(my_group + dy, side)
        else:
            group = lax.rem(my_group + 1 + k, groups)
        data = got_ref[pl.ds(pl.multiple_of(group * samples, 8), samples), :]
        chosen = mark_ref[0:nsrc, :]
        for m in range(0, samples, 2):
            both = [chosen * data[n : n + 1] for n in (m, m + 1)]
            xbuf[m * nsrc : (m + 2) * nsrc, :] = jnp.concatenate(both, axis=0).astype(BF)
        sums = dot(xbuf[...], table_ref[...]).astype(BF)
        for half in range(2):
            other = half * groups + group
            lanes = slice(half * LANES, (half + 1) * LANES)
            sbuf[other, 0:head, :] = weight_own[:, lanes]
            sbuf[other, head : head + part_rows, :] = sums[:, lanes]

            @pl.when(other != row)
            def _():
                by_group(group, lambda rows: copy2(other, row, rows).start())

    recv2[row] = sbuf[row]

    @loop(0, n_src)
    def _(i):
        @pl.when(i > 0)
        def _():
            send_coef(i).wait_recv()

    @loop(0, n_src)
    def _(r):
        at = pl.ds(pl.multiple_of(r * nsrc, 8), nsrc)
        c_ref[at, :] = crecv[r].astype(F32)[:nsrc]

    @loop(0, n_src)
    def _(i):
        r = row_at(i)

        @pl.when(i > 0)
        def _():
            by_group(my_group, lambda rows: copy2(r, r, rows).wait_recv())

        got = recv2[r].astype(F32)
        for m in range(samples):
            at = pl.ds(pl.multiple_of(m * all_src + r * nsrc, 8), nsrc)
            sf_ref[at, :] = got[head + m * nsrc : head + (m + 1) * nsrc]
        w2_ref[pl.ds(pl.multiple_of(r * nsrc, 8), nsrc), :] = got[:nsrc]

    coef = c_ref[...]
    turned = coef.T[:HALF]
    turned_lo = turned.astype(BF)
    square_hi, square_lo = split(turned * turned)
    coef_all = coef[:, :HALF].astype(BF)
    weight_lo = w2_ref[...].astype(BF)
    diag = dot(square_hi, weight_lo) + dot(square_lo, weight_lo)
    scale = 1.0 / (diag + damping)

    def by_samples(act):
        for m in range(last_samples):
            act(m)

        @pl.when(my_group < groups - 1)
        def _():
            for m in range(last_samples, samples):
                act(m)

    def refine(m):
        base = dk_ref[m * HALF : (m + 1) * HALF, :]
        sums = sf_ref[m * all_src : (m + 1) * all_src, :]
        resid = (sums - w2_ref[...] * dot(coef_all, base.astype(BF))).astype(BF)
        refined = (base + dot(turned_lo, resid) * scale).astype(BF).astype(F32)
        emap[m] = refined
        dk_ref[m * NCOEF : (m + 1) * NCOEF, :] = refined[:NCOEF]

    by_samples(refine)
    if owner_rows < eflat.shape[0]:
        dk_ref[owner_rows : eflat.shape[0], :] = jnp.zeros((eflat.shape[0] - owner_rows, LANES), F32)
    eflat[...] = dk_ref[0 : eflat.shape[0], :].astype(BF)

    px, py = row // side, row % side
    part_piece = half_rows // 2

    def at_offset(half, first, second):
        dx, dy = (first, second) if half == 0 else (second, first)
        return lax.rem(px + dx, side) * side + lax.rem(py + dy, side)

    def pass_on(half, origin, sub, target, key):
        if sub is None:
            rows = pl.ds(half * half_rows, half_rows)
        else:
            rows = pl.ds(half * half_rows + sub * part_piece, part_piece)
        return pltpu.make_async_remote_copy(
            src_ref=gbuf.at[origin, rows],
            dst_ref=gbuf.at[origin, rows],
            send_sem=ssem5.at[half, key[0], key[1]],
            recv_sem=rsem5.at[half, origin, sub or 0],
            device_id={"src": target},
            device_id_type=MESH,
        )

    def whole(half, origin):
        if half == 0 or last_samples * NCOEF > half_rows:
            return origin >= 0
        return origin % groups != groups - 1

    back, two = side - 1, side // 2
    ways = (1, back)
    relayed = (0, 1, back)

    def send_block(half, q):
        for n, way in enumerate(ways if q in relayed else (1, two, back)):
            pass_on(half, at_offset(half, q, 0), None, at_offset(half, 0, way), (q, n)).start()

    def arrived(half, origin, sub):
        pass_on(half, origin, sub, at_offset(half, 1, 0), (0, 0)).wait_recv()

    def relay(half, q):
        for n, way in enumerate(ways):
            origin = at_offset(half, q, (back, 1)[n])

            @pl.when(whole(half, origin))
            def _():
                arrived(half, origin, None)
                pass_on(half, origin, n, at_offset(half, 0, way), (q, 3 + n)).start()

    gbuf[row] = eflat[...]
    for half in range(2):

        @pl.when(whole(half, row))
        def _():
            for n, way in enumerate((two, 1, back)):
                pass_on(half, row, None, at_offset(half, way, 0), (side, n)).start()
            send_block(half, 0)

    gh_ref[...] = jnp.zeros_like(gh_ref)
    csq_ref[...] = jnp.zeros_like(csq_ref)
    blank = jnp.zeros((HALF, LANES), F32)

    def terms(m):
        refined = emap[m]
        sums = sf_ref[m * all_src : (m + 1) * all_src, :]
        resid = (sums - w2_ref[...] * dot(coef_all, refined.astype(BF))).astype(BF)
        gh_ref[...] += dot_nt(resid, jnp.concatenate([refined, blank], axis=0).astype(BF))
        csq_ref[...] += refined * refined

    by_samples(terms)
    curve_hi, curve_lo = split(jnp.concatenate([blank, csq_ref[...]], axis=0))
    weight_lo = w2_ref[...].astype(BF)
    gh_ref[...] += dot_nt(weight_lo, curve_hi) + dot_nt(weight_lo, curve_lo)

    def send3(i):
        return pltpu.make_async_remote_copy(
            src_ref=gh_ref.at[pl.ds(pl.multiple_of(row_at(i) * nsrc, 8), nsrc)],
            dst_ref=recv3.at[i],
            send_sem=ssem3.at[i],
            recv_sem=rsem3.at[i],
            device_id={"src": row_at(i)},
            device_id_type=MESH,
        )

    @loop(1, n_src)
    def _(i):
        send3(i).start()

    def forward(q):
        for half in range(2):
            origin = at_offset(half, q, 0)

            @pl.when(whole(half, origin))
            def _():
                arrived(half, origin, None)
                send_block(half, q)

    def ring(q):
        for half in range(2):
            relay(half, q)

    forward(1)
    forward(back)
    ring(0)
    forward(two)
    g1_ref[...] = gh_ref[pl.ds(pl.multiple_of(row * nsrc, 8), nsrc), :]

    @loop(1, n_src)
    def _(i):
        send3(i).wait_recv()
        g1_ref[...] += recv3[i]

    def send4(i):
        return pltpu.make_async_remote_copy(
            src_ref=g1_ref,
            dst_ref=recv4.at[me],
            send_sem=ssem4.at[i],
            recv_sem=rsem4.at[i],
            device_id={"unit": unit_at(i)},
            device_id_type=MESH,
        )

    @loop(1, n_unit)
    def _(i):
        send4(i).start()

    ring(1)
    ring(back)

    for q in range(side):
        for half in range(2):
            for way in (two,) if q in relayed else (1, back, two):
                origin = at_offset(half, q, way)

                @pl.when(whole(half, origin))
                def _():
                    for sub in (0, 1) if q in relayed else (None,):
                        arrived(half, origin, sub)

    for half in range(2):
        lanes = slice(half * LANES, (half + 1) * LANES)

        @loop(0, groups - 1)
        def _(group):
            at = pl.ds(pl.multiple_of(group * owner_rows, 8), owner_rows)
            out_ref[at, lanes] = gbuf[half * groups + group][:owner_rows]

        done_rows = (groups - 1) * owner_rows
        out_ref[done_rows:flat, lanes] = gbuf[half * groups + groups - 1][: flat - done_rows]

    recv4[me] = g1_ref[...]

    @loop(1, n_unit)
    def _(i):
        send4(i).wait_recv()

    total = recv4[0]
    for j in range(1, n_unit):
        total = total + recv4[j]
    step = total / (pltpu.roll(total, HALF, 1) + damping)
    nc_ref[...] = coef_ref[...] + step[:, :NCOEF]

    @loop(1, n_unit)
    def _(i):
        send1(i).wait_send()
        send4(i).wait_send()

    @loop(1, n_src)
    def _(i):
        send_coef(i).wait_send()
        send3(i).wait_send()
        other = row_at(i)
        by_group(other % groups, lambda rows: copy2(other, row, rows).wait_send())

    for half in range(2):
        for q in range(side):

            @pl.when(whole(half, at_offset(half, q, 0)))
            def _():
                for n in range(2 if q in relayed else 3):
                    pass_on(half, row, None, at_offset(half, 1, 0), (q, n)).wait_send()

            if q in relayed:
                for n in range(2):

                    @pl.when(whole(half, at_offset(half, q, (back, 1)[n])))
                    def _():
                        pass_on(half, row, n, at_offset(half, 1, 0), (q, 3 + n)).wait_send()

        @pl.when(whole(half, row))
        def _():
            for n in range(3):
                pass_on(half, row, None, at_offset(half, 1, 0), (side, n)).wait_send()


def body(coeffs, spectra, epoch_weight, source_blocks, epoch_owner, epoch_unit_local, design):
    n_src = lax.axis_size("src")
    n_unit = lax.axis_size("unit")
    epochs = spectra.shape[0]
    nblocks = epochs // BLOCK
    nsrc = coeffs.shape[0]
    units, flat = design.shape
    groups = n_src // 2
    samples = HALF // groups
    part_rows = samples * nsrc
    message = part_rows + up(nsrc, 16)
    all_src = n_src * nsrc
    side = math.isqrt(n_src)
    erows = up(samples * NCOEF, 64)
    vmem = pl.BlockSpec(memory_space=pltpu.VMEM)
    hbm = pl.BlockSpec(memory_space=pltpu.HBM)
    sems = pltpu.SemaphoreType.DMA
    new_design, new_coeffs = pl.pallas_call(
        functools.partial(kernel, n_src, n_unit, nsrc),
        out_shape=(
            jax.ShapeDtypeStruct((flat, units), BF),
            jax.ShapeDtypeStruct(coeffs.shape, F32),
        ),
        in_specs=[hbm] * 7,
        out_specs=(vmem, vmem),
        scratch_shapes=[
            pltpu.VMEM((NSAMP, epochs), BF),
            pltpu.VMEM((nblocks, BLOCK), BF),
            pltpu.VMEM((nblocks, BLOCK), jnp.int32),
            pltpu.VMEM((nblocks, BLOCK), jnp.int32),
            pltpu.VMEM((1, nsrc), jnp.int32),
            pltpu.VMEM(coeffs.shape, F32),
            pltpu.VMEM((flat, units), BF),
            pltpu.VMEM((n_unit * nblocks, LANES), F32),
            pltpu.VMEM((HALF, epochs), BF),
            pltpu.VMEM((SLOTS, epochs), BF),
            pltpu.VMEM((n_unit, HALF, SLOTS), BF),
            pltpu.VMEM((n_unit, HALF, SLOTS), BF),
            pltpu.VMEM((up(nsrc, 16), LANES), BF),
            pltpu.VMEM((n_src, up(nsrc, 16), LANES), BF),
            pltpu.VMEM((all_src, LANES), F32),
            pltpu.VMEM((samples * HALF, LANES), F32),
            pltpu.VMEM((n_unit * SLOTS, units), BF),
            pltpu.VMEM((up(nsrc, 16), n_unit * SLOTS), F32),
            pltpu.VMEM((HALF, n_unit * SLOTS), F32),
            pltpu.VMEM((part_rows, n_unit * SLOTS), BF),
            pltpu.VMEM((n_src, message, LANES), BF),
            pltpu.VMEM((n_src, message, LANES), BF),
            pltpu.VMEM((n_src * part_rows, LANES), F32),
            pltpu.VMEM((all_src, LANES), F32),
            pltpu.VMEM((samples, HALF, LANES), F32),
            pltpu.VMEM((erows, LANES), BF),
            pltpu.VMEM((n_src, erows, LANES), BF),
            pltpu.VMEM((all_src, LANES), F32),
            pltpu.VMEM((HALF, LANES), F32),
            pltpu.VMEM((n_src, nsrc, LANES), F32),
            pltpu.VMEM((nsrc, LANES), F32),
            pltpu.VMEM((n_unit, nsrc, LANES), F32),
            sems((7,)),
            sems((n_src,)),
            sems((n_src,)),
            sems((n_unit,)),
            sems((n_unit,)),
            sems((n_src,)),
            sems((n_src,)),
            sems((n_src,)),
            sems((n_src,)),
            sems((n_unit,)),
            sems((n_unit,)),
            sems((2, side + 1, 5)),
            sems((2, n_src, 2)),
        ],
        compiler_params=pltpu.CompilerParams(
            collective_id=0, has_side_effects=True, vmem_limit_bytes=44 * 1024 * 1024
        ),
    )(
        *[
            pltpu.with_memory_space_constraint(x, pltpu.HBM)
            for x in (
                spectra.T,
                epoch_weight.reshape(nblocks, BLOCK),
                epoch_unit_local.reshape(nblocks, BLOCK),
                epoch_owner.reshape(nblocks, BLOCK),
                source_blocks,
                coeffs,
                design.T,
            )
        ]
    )
    return (new_design.T.astype(F32), new_coeffs)


def solution(mesh):
    return jax.shard_map(
        body,
        mesh=mesh,
        in_specs=(
            P("src", None),
            P(("src", "unit"), None),
            P(("src", "unit")),
            P("src", None),
            P(("src", "unit"), None),
            P(("src", "unit")),
            P("unit", None),
        ),
        out_specs=(P("unit", None), P("src", None)),
        check_vma=False,
    )
```

```python
import functools
import math

import jax
import jax.numpy as jnp
from jax import lax
from jax.experimental import pallas as pl
from jax.experimental.pallas import tpu as pltpu
from jax.sharding import PartitionSpec as P

NCOEF = 55
NSAMP = 60
HALF = 64
LANES = 128
BLOCK = 128
SLOTS = 256
damping = 1.0

MESH = pl.DeviceIdType.MESH
BF = jnp.bfloat16
F32 = jnp.float32


def dot(a, b):
    return jnp.dot(a, b, preferred_element_type=F32)


def dot_nt(a, b):
    return lax.dot_general(a, b, (((1,), (1,)), ((), ())), preferred_element_type=F32)


def iota(shape, dim):
    return lax.broadcasted_iota(jnp.int32, shape, dim)


def ones_where(mask):
    return jnp.where(mask, 1.0, 0.0).astype(BF)


def split(x):
    high = x.astype(BF)
    return high, (x - high.astype(F32)).astype(BF)


def up(x, n):
    return -(-x // n) * n


def kernel(
    n_src,
    n_unit,
    nsrc,
    spec_hbm,
    w_hbm,
    u_hbm,
    o_hbm,
    cnt_hbm,
    coef_hbm,
    design_hbm,
    gbuf,
    nc_ref,
    spec_ref,
    w_ref,
    u_ref,
    o_ref,
    cnt_ref,
    coef_ref,
    dbuf,
    rank_ref,
    items_ref,
    place_ref,
    out1,
    recv1,
    cown,
    crecv,
    c_ref,
    dk_ref,
    table_ref,
    mark_ref,
    got_ref,
    xbuf,
    sbuf,
    recv2,
    sf_ref,
    ahead_ref,
    w2_ref,
    emap,
    eflat,
    gh_ref,
    csq_ref,
    recv3,
    g1_ref,
    recv4,
    lsem,
    csem,
    crsem,
    ssem1,
    rsem1,
    ssem2,
    rsem2,
    ssem3,
    rsem3,
    ssem4,
    rsem4,
    ssem5,
    rsem5,
):
    row = lax.axis_index("src")
    me = lax.axis_index("unit")
    epochs = spec_ref.shape[1]
    nblocks = epochs // BLOCK
    units = 2 * LANES
    groups = n_src // 2
    samples = HALF // groups
    part_rows = samples * nsrc
    all_src = n_src * nsrc
    head = up(nsrc, 16)
    last_samples = NSAMP - (groups - 1) * samples
    side = math.isqrt(n_src)
    flat = dbuf.shape[0]
    owner_rows = samples * NCOEF
    half_rows = eflat.shape[0] // 2
    my_half, my_group = row // groups, row % groups

    def unit_at(i):
        return lax.rem(me + i, n_unit)

    def row_at(i):
        return lax.rem(row + i, n_src)

    def loop(lo, hi):
        return pl.loop(lo, hi)

    barrier = pltpu.get_barrier_semaphore()

    @loop(1, n_unit)
    def _(i):
        pl.semaphore_signal(barrier, inc=1, device_id={"unit": unit_at(i)}, device_id_type=MESH)

    @loop(1, n_src)
    def _(i):
        pl.semaphore_signal(barrier, inc=1, device_id={"src": row_at(i)}, device_id_type=MESH)

    loads = [
        pltpu.make_async_copy(a, b, lsem.at[n])
        for n, (a, b) in enumerate(
            [
                (o_hbm, o_ref),
                (cnt_hbm, cnt_ref),
                (w_hbm, w_ref),
                (u_hbm, u_ref),
                (spec_hbm, spec_ref),
                (coef_hbm, coef_ref),
                (design_hbm, dbuf),
            ]
        )
    ]
    for load in loads:
        load.start()
    for load in loads[:-1]:
        load.wait()

    owner = o_ref[...]
    marks = jnp.concatenate([jnp.where(owner == j, 1.0, 0.0) for j in range(n_unit)], axis=0)
    marks_lo = marks.astype(BF)
    earlier = ones_where(iota((LANES, LANES), 0) < iota((LANES, LANES), 1))
    inside = dot(marks_lo, earlier)
    totals = dot(marks_lo, jnp.ones((LANES, LANES), BF)).astype(BF)
    nrow = n_unit * nblocks
    a, b = iota((nrow, nrow), 0), iota((nrow, nrow), 1)
    before = ones_where((a // nblocks == b // nblocks) & (b < a))
    rank_ref[...] = jnp.where(marks > 0.0, inside + dot(before, totals), -1.0)

    count = jnp.broadcast_to(cnt_ref[...].astype(F32), (nblocks, nsrc)).astype(BF)
    upto = ones_where(iota((nsrc, LANES), 0) <= iota((nsrc, LANES), 1))
    cum = dot(count, upto)
    index = (me * nblocks + iota((nblocks, LANES), 0)).astype(F32)
    done = ones_where((cum <= index) & (iota((nblocks, LANES), 1) < nsrc))
    source = dot(done, jnp.ones((LANES, LANES), BF))
    weights, locals_ = w_ref[...].astype(F32), u_ref[...].astype(F32)

    def one_row(x):
        return jnp.concatenate([x[b : b + 1, :] for b in range(nblocks)], axis=1)

    spare = jnp.zeros((HALF - NSAMP - 3, epochs), F32)
    items_ref[0:48, :] = spec_ref[0:48, :]
    items_ref[48:64, :] = jnp.concatenate(
        [
            spec_ref[48:NSAMP, :].astype(F32),
            one_row(weights),
            one_row(locals_),
            one_row(source),
            spare,
        ],
        axis=0,
    ).astype(BF)

    coef_lo = coef_ref[...].astype(BF)
    widen = ones_where(iota((NCOEF, LANES), 0) == iota((NCOEF, LANES), 1))
    deepen = ones_where(iota((cown.shape[0], nsrc), 0) == iota((cown.shape[0], nsrc), 1))
    padded = dot(deepen, dot(coef_lo, widen).astype(BF)).astype(BF)
    cown[...] = padded
    crecv[row] = padded

    pl.semaphore_wait(barrier, n_unit + n_src - 2)

    def send1(i):
        return pltpu.make_async_remote_copy(
            src_ref=out1.at[i],
            dst_ref=recv1.at[i],
            send_sem=ssem1.at[i],
            recv_sem=rsem1.at[i],
            device_id={"unit": unit_at(i)},
            device_id_type=MESH,
        )

    def send_coef(i):
        return pltpu.make_async_remote_copy(
            src_ref=cown,
            dst_ref=crecv.at[row],
            send_sem=csem.at[i],
            recv_sem=crsem.at[i],
            device_id={"src": row_at(i)},
            device_id_type=MESH,
        )

    def far_first(k):
        middle = n_unit // 2
        return lax.rem(middle + jnp.where(k % 2 == 1, (k + 1) // 2, n_unit - k // 2), n_unit)

    slot = iota((SLOTS, LANES), 0).astype(F32).astype(BF)
    one, zero = jnp.ones((), BF), jnp.zeros((), BF)

    @loop(0, n_unit)
    def _(k):
        i = far_first(k)
        ranks = rank_ref[pl.ds(pl.multiple_of(unit_at(i) * nblocks, nblocks), nblocks), :]
        for block in range(nblocks):
            line = jnp.broadcast_to(ranks[block : block + 1, :], (SLOTS, LANES)).astype(BF)
            place_ref[:, block * BLOCK : (block + 1) * BLOCK] = jnp.where(line == slot, one, zero)
        result = dot_nt(items_ref[...], place_ref[...]).astype(BF)
        out1[i] = result

        @pl.when(i > 0)
        def _():
            send1(i).start()

    @loop(1, n_src)
    def _(i):
        send_coef(i).start()

    loads[-1].wait()
    window = up(owner_rows + 15, 16)
    first_row = my_group * owner_rows
    start = jnp.minimum(first_row // 16 * 16, (flat - window) // 16 * 16)
    tail = flat // 16 * 16
    lanes_half = pl.ds(pl.multiple_of(my_half * LANES, LANES), LANES)
    shape = (samples * HALF, window)
    want = iota(shape, 0) // HALF * NCOEF + iota(shape, 0) % HALF + first_row
    real = iota(shape, 0) % HALF < NCOEF
    pick = ones_where(real & (want == iota(shape, 1) + start))
    maps = dot(pick, dbuf[pl.ds(pl.multiple_of(start, 16), window), lanes_half])
    shape = (samples * HALF, flat - tail)
    want = iota(shape, 0) // HALF * NCOEF + iota(shape, 0) % HALF + first_row
    real = iota(shape, 0) % HALF < NCOEF
    late = iota(shape, 1) + tail
    pick = ones_where(real & (want == late) & (late >= start + window))
    dk_ref[...] = maps + dot(pick, dbuf[tail:flat, lanes_half])

    unit_row = iota((units, SLOTS), 0).astype(F32)
    source_row = iota((mark_ref.shape[0], SLOTS), 0).astype(F32)
    recv1[0] = out1[0]

    @loop(0, n_unit)
    def _(k):
        i = jnp.where(k == 0, 0, far_first(k - 1))

        @pl.when(i > 0)
        def _():
            send1(i).wait_recv()

        got = recv1[i].astype(F32)
        at = pl.ds(pl.multiple_of(i * SLOTS, SLOTS), SLOTS)
        wrow = jnp.broadcast_to(got[60:61], (units, SLOTS))
        urow = jnp.broadcast_to(got[61:62], (units, SLOTS))
        srow = got[62:63]
        table_ref[at, :] = jnp.where(unit_row == urow, wrow, 0.0).T.astype(BF)
        chosen = jnp.broadcast_to(srow, source_row.shape) == source_row
        mark_ref[:, at] = jnp.where(chosen, 1.0, 0.0)
        got_ref[:, at] = got

    weight_own = dot(mark_ref[...].astype(BF), table_ref[...]).astype(BF)

    def copy2(other, slot, rows):
        return pltpu.make_async_remote_copy(
            src_ref=sbuf.at[other, pl.ds(0, rows)],
            dst_ref=recv2.at[slot, pl.ds(0, rows)],
            send_sem=ssem2.at[other],
            recv_sem=rsem2.at[slot],
            device_id={"src": other},
            device_id_type=MESH,
        )

    def by_group(group, act):
        @pl.when(group < groups - 1)
        def _():
            act(head + part_rows)

        @pl.when(group == groups - 1)
        def _():
            act(head + last_samples * nsrc)

    @loop(0, groups)
    def _(k):
        if side == 4:
            turn = lax.rem(k, 4)
            dy = jnp.where(turn == 0, 2, jnp.where(turn == 1, 1, jnp.where(turn == 2, 3, 0)))
            dx = jnp.where(k < 4, jnp.where(k == 1, 0, 1), jnp.where(k == 5, 1, 0))
            group = lax.rem(my_group // side + dx, 2) * side + lax.rem(my_group + dy, side)
        else:
            group = lax.rem(my_group + 1 + k, groups)
        data = got_ref[pl.ds(pl.multiple_of(group * samples, 8), samples), :]
        chosen = mark_ref[0:nsrc, :]
        for m in range(0, samples, 2):
            both = [chosen * data[n : n + 1] for n in (m, m + 1)]
            xbuf[m * nsrc : (m + 2) * nsrc, :] = jnp.concatenate(both, axis=0).astype(BF)
        sums = dot(xbuf[...], table_ref[...]).astype(BF)
        for half in range(2):
            other = half * groups + group
            lanes = slice(half * LANES, (half + 1) * LANES)
            sbuf[other, 0:head, :] = weight_own[:, lanes]
            sbuf[other, head : head + part_rows, :] = sums[:, lanes]

            @pl.when(other != row)
            def _():
                by_group(group, lambda rows: copy2(other, row, rows).start())

    recv2[row] = sbuf[row]

    @loop(0, n_src)
    def _(i):
        @pl.when(i > 0)
        def _():
            send_coef(i).wait_recv()

    @loop(0, n_src)
    def _(r):
        at = pl.ds(pl.multiple_of(r * nsrc, 8), nsrc)
        c_ref[at, :] = crecv[r].astype(F32)[:nsrc]

    coef = c_ref[...]
    turned = coef.T[:HALF]
    turned_lo = turned.astype(BF)
    square_hi, square_lo = split(turned * turned)
    coef_all = coef[:, :HALF].astype(BF)
    for m in range(samples):
        ahead_ref[m] = dot(coef_all, dk_ref[m * HALF : (m + 1) * HALF, :].astype(BF))

    @loop(0, n_src)
    def _(i):
        r = row_at(i)

        @pl.when(i > 0)
        def _():
            by_group(my_group, lambda rows: copy2(r, r, rows).wait_recv())

        got = recv2[r].astype(F32)
        for m in range(samples):
            at = pl.ds(pl.multiple_of(m * all_src + r * nsrc, 8), nsrc)
            sf_ref[at, :] = got[head + m * nsrc : head + (m + 1) * nsrc]
        w2_ref[pl.ds(pl.multiple_of(r * nsrc, 8), nsrc), :] = got[:nsrc]

    weight_lo = w2_ref[...].astype(BF)
    diag = dot(square_hi, weight_lo) + dot(square_lo, weight_lo)
    scale = 1.0 / (diag + damping)

    def by_samples(act):
        for m in range(last_samples):
            act(m)

        @pl.when(my_group < groups - 1)
        def _():
            for m in range(last_samples, samples):
                act(m)

    def refine(m):
        base = dk_ref[m * HALF : (m + 1) * HALF, :]
        sums = sf_ref[m * all_src : (m + 1) * all_src, :]
        resid = (sums - w2_ref[...] * ahead_ref[m]).astype(BF)
        refined = (base + dot(turned_lo, resid) * scale).astype(BF).astype(F32)
        emap[m] = refined
        dk_ref[m * NCOEF : (m + 1) * NCOEF, :] = refined[:NCOEF]

    by_samples(refine)
    if owner_rows < eflat.shape[0]:
        dk_ref[owner_rows : eflat.shape[0], :] = jnp.zeros((eflat.shape[0] - owner_rows, LANES), F32)
    eflat[...] = dk_ref[0 : eflat.shape[0], :].astype(BF)

    px, py = row // side, row % side
    part_piece = half_rows // 2

    def at_offset(half, first, second):
        dx, dy = (first, second) if half == 0 else (second, first)
        return lax.rem(px + dx, side) * side + lax.rem(py + dy, side)

    def pass_on(half, origin, sub, target, key):
        if sub is None:
            rows = pl.ds(half * half_rows, half_rows)
        else:
            rows = pl.ds(half * half_rows + sub * part_piece, part_piece)
        return pltpu.make_async_remote_copy(
            src_ref=gbuf.at[origin, rows],
            dst_ref=gbuf.at[origin, rows],
            send_sem=ssem5.at[half, key[0], key[1]],
            recv_sem=rsem5.at[half, origin, sub or 0],
            device_id={"src": target},
            device_id_type=MESH,
        )

    def whole(half, origin):
        if half == 0 or last_samples * NCOEF > half_rows:
            return origin >= 0
        return origin % groups != groups - 1

    back, two = side - 1, side // 2
    ways = (1, back)
    relayed = (0, 1, back)

    def send_block(half, q):
        for n, way in enumerate(ways if q in relayed else (1, two, back)):
            pass_on(half, at_offset(half, q, 0), None, at_offset(half, 0, way), (q, n)).start()

    def arrived(half, origin, sub):
        pass_on(half, origin, sub, at_offset(half, 1, 0), (0, 0)).wait_recv()

    def relay(half, q):
        for n, way in enumerate(ways):
            origin = at_offset(half, q, (back, 1)[n])

            @pl.when(whole(half, origin))
            def _():
                arrived(half, origin, None)
                pass_on(half, origin, n, at_offset(half, 0, way), (q, 3 + n)).start()

    gbuf[row] = eflat[...]
    for half in range(2):

        @pl.when(whole(half, row))
        def _():
            for n, way in enumerate((two, 1, back)):
                pass_on(half, row, None, at_offset(half, way, 0), (side, n)).start()
            send_block(half, 0)

    gh_ref[...] = jnp.zeros_like(gh_ref)
    csq_ref[...] = jnp.zeros_like(csq_ref)
    blank = jnp.zeros((HALF, LANES), F32)

    def terms(m):
        refined = emap[m]
        sums = sf_ref[m * all_src : (m + 1) * all_src, :]
        resid = (sums - w2_ref[...] * dot(coef_all, refined.astype(BF))).astype(BF)
        gh_ref[...] += dot_nt(resid, jnp.concatenate([refined, blank], axis=0).astype(BF))
        csq_ref[...] += refined * refined

    by_samples(terms)
    curve_hi, curve_lo = split(jnp.concatenate([blank, csq_ref[...]], axis=0))
    weight_lo = w2_ref[...].astype(BF)
    gh_ref[...] += dot_nt(weight_lo, curve_hi) + dot_nt(weight_lo, curve_lo)

    def send3(i):
        return pltpu.make_async_remote_copy(
            src_ref=gh_ref.at[pl.ds(pl.multiple_of(row_at(i) * nsrc, 8), nsrc)],
            dst_ref=recv3.at[i],
            send_sem=ssem3.at[i],
            recv_sem=rsem3.at[i],
            device_id={"src": row_at(i)},
            device_id_type=MESH,
        )

    @loop(1, n_src)
    def _(i):
        send3(i).start()

    def forward(q):
        for half in range(2):
            origin = at_offset(half, q, 0)

            @pl.when(whole(half, origin))
            def _():
                arrived(half, origin, None)
                send_block(half, q)

    def ring(q):
        for half in range(2):
            relay(half, q)

    forward(1)
    forward(back)
    ring(0)
    forward(two)
    g1_ref[...] = gh_ref[pl.ds(pl.multiple_of(row * nsrc, 8), nsrc), :]

    @loop(1, n_src)
    def _(i):
        send3(i).wait_recv()
        g1_ref[...] += recv3[i]

    def send4(i):
        return pltpu.make_async_remote_copy(
            src_ref=g1_ref,
            dst_ref=recv4.at[me],
            send_sem=ssem4.at[i],
            recv_sem=rsem4.at[i],
            device_id={"unit": unit_at(i)},
            device_id_type=MESH,
        )

    @loop(1, n_unit)
    def _(i):
        send4(i).start()

    ring(1)
    ring(back)

    for q in range(side):
        for half in range(2):
            for way in (two,) if q in relayed else (1, back, two):
                origin = at_offset(half, q, way)

                @pl.when(whole(half, origin))
                def _():
                    for sub in (0, 1) if q in relayed else (None,):
                        arrived(half, origin, sub)

    recv4[me] = g1_ref[...]

    @loop(1, n_unit)
    def _(i):
        send4(i).wait_recv()

    total = recv4[0]
    for j in range(1, n_unit):
        total = total + recv4[j]
    step = total / (pltpu.roll(total, HALF, 1) + damping)
    nc_ref[...] = coef_ref[...] + step[:, :NCOEF]

    @loop(1, n_unit)
    def _(i):
        send1(i).wait_send()
        send4(i).wait_send()

    @loop(1, n_src)
    def _(i):
        send_coef(i).wait_send()
        send3(i).wait_send()
        other = row_at(i)
        by_group(other % groups, lambda rows: copy2(other, row, rows).wait_send())

    for half in range(2):
        for q in range(side):

            @pl.when(whole(half, at_offset(half, q, 0)))
            def _():
                for n in range(2 if q in relayed else 3):
                    pass_on(half, row, None, at_offset(half, 1, 0), (q, n)).wait_send()

            if q in relayed:
                for n in range(2):

                    @pl.when(whole(half, at_offset(half, q, (back, 1)[n])))
                    def _():
                        pass_on(half, row, n, at_offset(half, 1, 0), (q, 3 + n)).wait_send()

        @pl.when(whole(half, row))
        def _():
            for n in range(3):
                pass_on(half, row, None, at_offset(half, 1, 0), (side, n)).wait_send()


def widen_kernel(step, in_ref, nc_in, out_hbm, nc_hbm, wide_ref, sems):
    groups = in_ref.shape[0] // 2
    flat = wide_ref.shape[0]
    copies = [pltpu.make_async_copy(nc_in, nc_hbm, sems.at[groups])]
    copies[0].start()
    for group in range(groups):
        first, last = group * step, min((group + 1) * step, flat)
        for half in range(2):
            lanes = slice(half * LANES, (half + 1) * LANES)
            wide_ref[first:last, lanes] = in_ref[half * groups + group].astype(F32)[: last - first]
        rows = pl.ds(first, last - first)
        copies.append(pltpu.make_async_copy(wide_ref.at[rows], out_hbm.at[rows], sems.at[group]))
        copies[-1].start()
    for copy in copies:
        copy.wait()


def widen(gathered, new_coeffs, flat, step):
    vmem = pl.BlockSpec(memory_space=pltpu.VMEM)
    hbm = pl.BlockSpec(memory_space=pltpu.HBM)
    return pl.pallas_call(
        functools.partial(widen_kernel, step),
        out_shape=(
            jax.ShapeDtypeStruct((flat, 2 * LANES), F32),
            jax.ShapeDtypeStruct(new_coeffs.shape, F32),
        ),
        in_specs=[vmem, vmem],
        out_specs=(hbm, hbm),
        scratch_shapes=[
            pltpu.VMEM((flat, 2 * LANES), F32),
            pltpu.SemaphoreType.DMA((gathered.shape[0] // 2 + 1,)),
        ],
        compiler_params=pltpu.CompilerParams(vmem_limit_bytes=16 * 1024 * 1024),
    )(gathered, new_coeffs)


def body(coeffs, spectra, epoch_weight, source_blocks, epoch_owner, epoch_unit_local, design):
    n_src = lax.axis_size("src")
    n_unit = lax.axis_size("unit")
    epochs = spectra.shape[0]
    nblocks = epochs // BLOCK
    nsrc = coeffs.shape[0]
    units, flat = design.shape
    groups = n_src // 2
    samples = HALF // groups
    part_rows = samples * nsrc
    message = part_rows + up(nsrc, 16)
    all_src = n_src * nsrc
    side = math.isqrt(n_src)
    erows = up(samples * NCOEF, 64)
    vmem = pl.BlockSpec(memory_space=pltpu.VMEM)
    hbm = pl.BlockSpec(memory_space=pltpu.HBM)
    sems = pltpu.SemaphoreType.DMA
    gathered, new_coeffs = pl.pallas_call(
        functools.partial(kernel, n_src, n_unit, nsrc),
        out_shape=(
            jax.ShapeDtypeStruct((n_src, erows, LANES), BF),
            jax.ShapeDtypeStruct(coeffs.shape, F32),
        ),
        in_specs=[hbm] * 7,
        out_specs=(vmem, vmem),
        scratch_shapes=[
            pltpu.VMEM((NSAMP, epochs), BF),
            pltpu.VMEM((nblocks, BLOCK), BF),
            pltpu.VMEM((nblocks, BLOCK), jnp.int32),
            pltpu.VMEM((nblocks, BLOCK), jnp.int32),
            pltpu.VMEM((1, nsrc), jnp.int32),
            pltpu.VMEM(coeffs.shape, F32),
            pltpu.VMEM((flat, units), BF),
            pltpu.VMEM((n_unit * nblocks, LANES), F32),
            pltpu.VMEM((HALF, epochs), BF),
            pltpu.VMEM((SLOTS, epochs), BF),
            pltpu.VMEM((n_unit, HALF, SLOTS), BF),
            pltpu.VMEM((n_unit, HALF, SLOTS), BF),
            pltpu.VMEM((up(nsrc, 16), LANES), BF),
            pltpu.VMEM((n_src, up(nsrc, 16), LANES), BF),
            pltpu.VMEM((all_src, LANES), F32),
            pltpu.VMEM((samples * HALF, LANES), F32),
            pltpu.VMEM((n_unit * SLOTS, units), BF),
            pltpu.VMEM((up(nsrc, 16), n_unit * SLOTS), F32),
            pltpu.VMEM((HALF, n_unit * SLOTS), F32),
            pltpu.VMEM((part_rows, n_unit * SLOTS), BF),
            pltpu.VMEM((n_src, message, LANES), BF),
            pltpu.VMEM((n_src, message, LANES), BF),
            pltpu.VMEM((n_src * part_rows, LANES), F32),
            pltpu.VMEM((samples, all_src, LANES), F32),
            pltpu.VMEM((all_src, LANES), F32),
            pltpu.VMEM((samples, HALF, LANES), F32),
            pltpu.VMEM((erows, LANES), BF),
            pltpu.VMEM((all_src, LANES), F32),
            pltpu.VMEM((HALF, LANES), F32),
            pltpu.VMEM((n_src, nsrc, LANES), F32),
            pltpu.VMEM((nsrc, LANES), F32),
            pltpu.VMEM((n_unit, nsrc, LANES), F32),
            sems((7,)),
            sems((n_src,)),
            sems((n_src,)),
            sems((n_unit,)),
            sems((n_unit,)),
            sems((n_src,)),
            sems((n_src,)),
            sems((n_src,)),
            sems((n_src,)),
            sems((n_unit,)),
            sems((n_unit,)),
            sems((2, side + 1, 5)),
            sems((2, n_src, 2)),
        ],
        compiler_params=pltpu.CompilerParams(
            collective_id=0, has_side_effects=True, vmem_limit_bytes=44 * 1024 * 1024
        ),
    )(
        *[
            pltpu.with_memory_space_constraint(x, pltpu.HBM)
            for x in (
                spectra.T,
                epoch_weight.reshape(nblocks, BLOCK),
                epoch_unit_local.reshape(nblocks, BLOCK),
                epoch_owner.reshape(nblocks, BLOCK),
                source_blocks,
                coeffs,
                design.T,
            )
        ]
    )
    new_design, new_coeffs = widen(gathered, new_coeffs, flat, samples * NCOEF)
    return (new_design.T, new_coeffs)


def solution(mesh):
    return jax.shard_map(
        body,
        mesh=mesh,
        in_specs=(
            P("src", None),
            P(("src", "unit"), None),
            P(("src", "unit")),
            P("src", None),
            P(("src", "unit"), None),
            P(("src", "unit")),
            P("unit", None),
        ),
        out_specs=(P("unit", None), P("src", None)),
        check_vma=False,
    )
```

```python
import functools
import math

import jax
import jax.numpy as jnp
from jax import lax
from jax.experimental import pallas as pl
from jax.experimental.pallas import tpu as pltpu
from jax.sharding import PartitionSpec as P

NCOEF = 55
NSAMP = 60
HALF = 64
LANES = 128
BLOCK = 128
SLOTS = 256
damping = 1.0

MESH = pl.DeviceIdType.MESH
BF = jnp.bfloat16
F32 = jnp.float32


def dot(a, b):
    return jnp.dot(a, b, preferred_element_type=F32)


def dot_nt(a, b):
    return lax.dot_general(a, b, (((1,), (1,)), ((), ())), preferred_element_type=F32)


def iota(shape, dim):
    return lax.broadcasted_iota(jnp.int32, shape, dim)


def ones_where(mask):
    return jnp.where(mask, 1.0, 0.0).astype(BF)


def split(x):
    high = x.astype(BF)
    return high, (x - high.astype(F32)).astype(BF)


def up(x, n):
    return -(-x // n) * n


def kernel(
    n_src,
    n_unit,
    nsrc,
    spec_hbm,
    w_hbm,
    u_hbm,
    o_hbm,
    cnt_hbm,
    coef_hbm,
    design_hbm,
    gbuf,
    nc_ref,
    spec_ref,
    w_ref,
    u_ref,
    o_ref,
    cnt_ref,
    coef_ref,
    dbuf,
    rank_ref,
    items_ref,
    place_ref,
    out1,
    recv1,
    cown,
    crecv,
    c_ref,
    dk_ref,
    table_ref,
    mark_ref,
    got_ref,
    xbuf,
    sbuf,
    recv2,
    sf_ref,
    ahead_ref,
    w2_ref,
    emap,
    eflat,
    gh_ref,
    csq_ref,
    recv3,
    g1_ref,
    recv4,
    lsem,
    csem,
    crsem,
    ssem1,
    rsem1,
    ssem2,
    rsem2,
    ssem3,
    rsem3,
    ssem4,
    rsem4,
    ssem5,
    rsem5,
    ready,
):
    row = lax.axis_index("src")
    me = lax.axis_index("unit")
    epochs = spec_ref.shape[1]
    nblocks = epochs // BLOCK
    units = 2 * LANES
    groups = n_src // 2
    samples = HALF // groups
    part_rows = samples * nsrc
    all_src = n_src * nsrc
    head = up(nsrc, 16)
    last_samples = NSAMP - (groups - 1) * samples
    side = math.isqrt(n_src)
    flat = dbuf.shape[0]
    owner_rows = samples * NCOEF
    half_rows = eflat.shape[0] // 2
    my_half, my_group = row // groups, row % groups

    def unit_at(i):
        return lax.rem(me + i, n_unit)

    def row_at(i):
        return lax.rem(row + i, n_src)

    def loop(lo, hi):
        return pl.loop(lo, hi)

    barrier = pltpu.get_barrier_semaphore()

    @loop(1, n_unit)
    def _(i):
        pl.semaphore_signal(barrier, inc=1, device_id={"unit": unit_at(i)}, device_id_type=MESH)

    px, py = row // side, row % side

    @loop(1, side)
    def _(i):
        across = lax.rem(px + i, side) * side + py
        along = px * side + lax.rem(py + i, side)
        pl.semaphore_signal(barrier, inc=1, device_id={"src": across}, device_id_type=MESH)
        pl.semaphore_signal(barrier, inc=1, device_id={"src": along}, device_id_type=MESH)

    loads = [
        pltpu.make_async_copy(a, b, lsem.at[n])
        for n, (a, b) in enumerate(
            [
                (o_hbm, o_ref),
                (cnt_hbm, cnt_ref),
                (w_hbm, w_ref),
                (u_hbm, u_ref),
                (spec_hbm, spec_ref),
                (coef_hbm, coef_ref),
                (design_hbm, dbuf),
            ]
        )
    ]
    for load in loads:
        load.start()
    for load in loads[:-1]:
        load.wait()

    owner = o_ref[...]
    marks = jnp.concatenate([jnp.where(owner == j, 1.0, 0.0) for j in range(n_unit)], axis=0)
    marks_lo = marks.astype(BF)
    earlier = ones_where(iota((LANES, LANES), 0) < iota((LANES, LANES), 1))
    inside = dot(marks_lo, earlier)
    totals = dot(marks_lo, jnp.ones((LANES, LANES), BF)).astype(BF)
    nrow = n_unit * nblocks
    a, b = iota((nrow, nrow), 0), iota((nrow, nrow), 1)
    before = ones_where((a // nblocks == b // nblocks) & (b < a))
    rank_ref[...] = jnp.where(marks > 0.0, inside + dot(before, totals), -1.0)

    count = jnp.broadcast_to(cnt_ref[...].astype(F32), (nblocks, nsrc)).astype(BF)
    upto = ones_where(iota((nsrc, LANES), 0) <= iota((nsrc, LANES), 1))
    cum = dot(count, upto)
    index = (me * nblocks + iota((nblocks, LANES), 0)).astype(F32)
    done = ones_where((cum <= index) & (iota((nblocks, LANES), 1) < nsrc))
    source = dot(done, jnp.ones((LANES, LANES), BF))
    weights, locals_ = w_ref[...].astype(F32), u_ref[...].astype(F32)

    def one_row(x):
        return jnp.concatenate([x[b : b + 1, :] for b in range(nblocks)], axis=1)

    spare = jnp.zeros((HALF - NSAMP - 3, epochs), F32)
    items_ref[0:48, :] = spec_ref[0:48, :]
    items_ref[48:64, :] = jnp.concatenate(
        [
            spec_ref[48:NSAMP, :].astype(F32),
            one_row(weights),
            one_row(locals_),
            one_row(source),
            spare,
        ],
        axis=0,
    ).astype(BF)

    coef_lo = coef_ref[...].astype(BF)
    widen = ones_where(iota((NCOEF, LANES), 0) == iota((NCOEF, LANES), 1))
    deepen = ones_where(iota((cown.shape[0], nsrc), 0) == iota((cown.shape[0], nsrc), 1))
    padded = dot(deepen, dot(coef_lo, widen).astype(BF)).astype(BF)
    cown[...] = padded
    crecv[row] = padded

    pl.semaphore_wait(barrier, n_unit - 1 + 2 * (side - 1))

    @loop(1, side)
    def _(i):
        along = px * side + lax.rem(py + i, side)
        pl.semaphore_signal(ready, inc=1, device_id={"src": along}, device_id_type=MESH)

    def send1(i):
        return pltpu.make_async_remote_copy(
            src_ref=out1.at[i],
            dst_ref=recv1.at[i],
            send_sem=ssem1.at[i],
            recv_sem=rsem1.at[i],
            device_id={"unit": unit_at(i)},
            device_id_type=MESH,
        )

    def send_coef(i):
        return pltpu.make_async_remote_copy(
            src_ref=cown,
            dst_ref=crecv.at[row],
            send_sem=csem.at[i],
            recv_sem=crsem.at[i],
            device_id={"src": row_at(i)},
            device_id_type=MESH,
        )

    def far_first(k):
        middle = n_unit // 2
        return lax.rem(middle + jnp.where(k % 2 == 1, (k + 1) // 2, n_unit - k // 2), n_unit)

    slot = iota((SLOTS, LANES), 0).astype(F32).astype(BF)
    one, zero = jnp.ones((), BF), jnp.zeros((), BF)

    @loop(0, n_unit)
    def _(k):
        i = far_first(k)
        ranks = rank_ref[pl.ds(pl.multiple_of(unit_at(i) * nblocks, nblocks), nblocks), :]
        for block in range(nblocks):
            line = jnp.broadcast_to(ranks[block : block + 1, :], (SLOTS, LANES)).astype(BF)
            place_ref[:, block * BLOCK : (block + 1) * BLOCK] = jnp.where(line == slot, one, zero)
        result = dot_nt(items_ref[...], place_ref[...]).astype(BF)
        out1[i] = result

        @pl.when(i > 0)
        def _():
            send1(i).start()

    pl.semaphore_wait(ready, side - 1)

    @loop(1, n_src)
    def _(i):
        send_coef(i).start()

    loads[-1].wait()
    window = up(owner_rows + 15, 16)
    first_row = my_group * owner_rows
    start = jnp.minimum(first_row // 16 * 16, (flat - window) // 16 * 16)
    tail = flat // 16 * 16
    lanes_half = pl.ds(pl.multiple_of(my_half * LANES, LANES), LANES)
    shape = (samples * HALF, window)
    want = iota(shape, 0) // HALF * NCOEF + iota(shape, 0) % HALF + first_row
    real = iota(shape, 0) % HALF < NCOEF
    pick = ones_where(real & (want == iota(shape, 1) + start))
    maps = dot(pick, dbuf[pl.ds(pl.multiple_of(start, 16), window), lanes_half])
    shape = (samples * HALF, flat - tail)
    want = iota(shape, 0) // HALF * NCOEF + iota(shape, 0) % HALF + first_row
    real = iota(shape, 0) % HALF < NCOEF
    late = iota(shape, 1) + tail
    pick = ones_where(real & (want == late) & (late >= start + window))
    dk_ref[...] = maps + dot(pick, dbuf[tail:flat, lanes_half])

    unit_row = iota((units, SLOTS), 0).astype(F32)
    source_row = iota((mark_ref.shape[0], SLOTS), 0).astype(F32)
    recv1[0] = out1[0]

    @loop(0, n_unit)
    def _(k):
        i = jnp.where(k == 0, 0, far_first(k - 1))

        @pl.when(i > 0)
        def _():
            send1(i).wait_recv()

        got = recv1[i].astype(F32)
        at = pl.ds(pl.multiple_of(i * SLOTS, SLOTS), SLOTS)
        wrow = jnp.broadcast_to(got[60:61], (units, SLOTS))
        urow = jnp.broadcast_to(got[61:62], (units, SLOTS))
        srow = got[62:63]
        table_ref[at, :] = jnp.where(unit_row == urow, wrow, 0.0).T.astype(BF)
        chosen = jnp.broadcast_to(srow, source_row.shape) == source_row
        mark_ref[:, at] = jnp.where(chosen, 1.0, 0.0)
        got_ref[:, at] = got

    weight_own = dot(mark_ref[...].astype(BF), table_ref[...]).astype(BF)

    def copy2(other, slot, rows):
        return pltpu.make_async_remote_copy(
            src_ref=sbuf.at[other, pl.ds(0, rows)],
            dst_ref=recv2.at[slot, pl.ds(0, rows)],
            send_sem=ssem2.at[other],
            recv_sem=rsem2.at[slot],
            device_id={"src": other},
            device_id_type=MESH,
        )

    def by_group(group, act):
        @pl.when(group < groups - 1)
        def _():
            act(head + part_rows)

        @pl.when(group == groups - 1)
        def _():
            act(head + last_samples * nsrc)

    @loop(0, groups)
    def _(k):
        if side == 4:
            turn = lax.rem(k, 4)
            dy = jnp.where(turn == 0, 2, jnp.where(turn == 1, 1, jnp.where(turn == 2, 3, 0)))
            dx = jnp.where(k < 4, jnp.where(k == 1, 0, 1), jnp.where(k == 5, 1, 0))
            group = lax.rem(my_group // side + dx, 2) * side + lax.rem(my_group + dy, side)
        else:
            group = lax.rem(my_group + 1 + k, groups)
        data = got_ref[pl.ds(pl.multiple_of(group * samples, 8), samples), :]
        chosen = mark_ref[0:nsrc, :]
        for m in range(0, samples, 2):
            both = [chosen * data[n : n + 1] for n in (m, m + 1)]
            xbuf[m * nsrc : (m + 2) * nsrc, :] = jnp.concatenate(both, axis=0).astype(BF)
        sums = dot(xbuf[...], table_ref[...]).astype(BF)
        for half in range(2):
            other = half * groups + group
            lanes = slice(half * LANES, (half + 1) * LANES)
            sbuf[other, 0:head, :] = weight_own[:, lanes]
            sbuf[other, head : head + part_rows, :] = sums[:, lanes]

            @pl.when(other != row)
            def _():
                by_group(group, lambda rows: copy2(other, row, rows).start())

    recv2[row] = sbuf[row]

    @loop(0, n_src)
    def _(i):
        @pl.when(i > 0)
        def _():
            send_coef(i).wait_recv()

    @loop(0, n_src)
    def _(r):
        at = pl.ds(pl.multiple_of(r * nsrc, 8), nsrc)
        c_ref[at, :] = crecv[r].astype(F32)[:nsrc]

    coef = c_ref[...]
    turned = coef.T[:HALF]
    turned_lo = turned.astype(BF)
    square_hi, square_lo = split(turned * turned)
    coef_all = coef[:, :HALF].astype(BF)
    for m in range(samples):
        ahead_ref[m] = dot(coef_all, dk_ref[m * HALF : (m + 1) * HALF, :].astype(BF))

    @loop(0, n_src)
    def _(i):
        r = row_at(i)

        @pl.when(i > 0)
        def _():
            by_group(my_group, lambda rows: copy2(r, r, rows).wait_recv())

        got = recv2[r].astype(F32)
        for m in range(samples):
            at = pl.ds(pl.multiple_of(m * all_src + r * nsrc, 8), nsrc)
            sf_ref[at, :] = got[head + m * nsrc : head + (m + 1) * nsrc]
        w2_ref[pl.ds(pl.multiple_of(r * nsrc, 8), nsrc), :] = got[:nsrc]

    weight_lo = w2_ref[...].astype(BF)
    diag = dot(square_hi, weight_lo) + dot(square_lo, weight_lo)
    scale = 1.0 / (diag + damping)

    def by_samples(act):
        for m in range(last_samples):
            act(m)

        @pl.when(my_group < groups - 1)
        def _():
            for m in range(last_samples, samples):
                act(m)

    def refine(m):
        base = dk_ref[m * HALF : (m + 1) * HALF, :]
        sums = sf_ref[m * all_src : (m + 1) * all_src, :]
        resid = (sums - w2_ref[...] * ahead_ref[m]).astype(BF)
        refined = (base + dot(turned_lo, resid) * scale).astype(BF).astype(F32)
        emap[m] = refined
        dk_ref[m * NCOEF : (m + 1) * NCOEF, :] = refined[:NCOEF]

    by_samples(refine)
    if owner_rows < eflat.shape[0]:
        dk_ref[owner_rows : eflat.shape[0], :] = jnp.zeros((eflat.shape[0] - owner_rows, LANES), F32)
    eflat[...] = dk_ref[0 : eflat.shape[0], :].astype(BF)

    part_piece = half_rows // 2

    def at_offset(half, first, second):
        dx, dy = (first, second) if half == 0 else (second, first)
        return lax.rem(px + dx, side) * side + lax.rem(py + dy, side)

    def pass_on(half, origin, sub, target, key):
        if sub is None:
            rows = pl.ds(half * half_rows, half_rows)
        else:
            rows = pl.ds(half * half_rows + sub * part_piece, part_piece)
        return pltpu.make_async_remote_copy(
            src_ref=gbuf.at[origin, rows],
            dst_ref=gbuf.at[origin, rows],
            send_sem=ssem5.at[half, key[0], key[1]],
            recv_sem=rsem5.at[half, origin, sub or 0],
            device_id={"src": target},
            device_id_type=MESH,
        )

    def whole(half, origin):
        if half == 0 or last_samples * NCOEF > half_rows:
            return origin >= 0
        return origin % groups != groups - 1

    back, two = side - 1, side // 2
    ways = (1, back)
    relayed = (0, 1, back)

    def send_block(half, q):
        for n, way in enumerate(ways if q in relayed else (1, two, back)):
            pass_on(half, at_offset(half, q, 0), None, at_offset(half, 0, way), (q, n)).start()

    def arrived(half, origin, sub):
        pass_on(half, origin, sub, at_offset(half, 1, 0), (0, 0)).wait_recv()

    def relay(half, q):
        for n, way in enumerate(ways):
            origin = at_offset(half, q, (back, 1)[n])

            @pl.when(whole(half, origin))
            def _():
                arrived(half, origin, None)
                pass_on(half, origin, n, at_offset(half, 0, way), (q, 3 + n)).start()

    gbuf[row] = eflat[...]
    for half in range(2):

        @pl.when(whole(half, row))
        def _():
            for n, way in enumerate((two, 1, back)):
                pass_on(half, row, None, at_offset(half, way, 0), (side, n)).start()

    for half in range(2):

        @pl.when(whole(half, row))
        def _():
            send_block(half, 0)

    gh_ref[...] = jnp.zeros_like(gh_ref)
    csq_ref[...] = jnp.zeros_like(csq_ref)
    blank = jnp.zeros((HALF, LANES), F32)

    def terms(m):
        refined = emap[m]
        sums = sf_ref[m * all_src : (m + 1) * all_src, :]
        resid = (sums - w2_ref[...] * dot(coef_all, refined.astype(BF))).astype(BF)
        gh_ref[...] += dot_nt(resid, jnp.concatenate([refined, blank], axis=0).astype(BF))
        csq_ref[...] += refined * refined

    by_samples(terms)
    curve_hi, curve_lo = split(jnp.concatenate([blank, csq_ref[...]], axis=0))
    weight_lo = w2_ref[...].astype(BF)
    gh_ref[...] += dot_nt(weight_lo, curve_hi) + dot_nt(weight_lo, curve_lo)

    def send3(i):
        return pltpu.make_async_remote_copy(
            src_ref=gh_ref.at[pl.ds(pl.multiple_of(row_at(i) * nsrc, 8), nsrc)],
            dst_ref=recv3.at[i],
            send_sem=ssem3.at[i],
            recv_sem=rsem3.at[i],
            device_id={"src": row_at(i)},
            device_id_type=MESH,
        )

    @loop(1, n_src)
    def _(i):
        send3(i).start()

    def forward(q):
        for half in range(2):
            origin = at_offset(half, q, 0)

            @pl.when(whole(half, origin))
            def _():
                arrived(half, origin, None)
                send_block(half, q)

    def ring(q):
        for half in range(2):
            relay(half, q)

    forward(1)
    forward(back)
    ring(0)
    forward(two)
    g1_ref[...] = gh_ref[pl.ds(pl.multiple_of(row * nsrc, 8), nsrc), :]

    @loop(1, n_src)
    def _(i):
        send3(i).wait_recv()
        g1_ref[...] += recv3[i]

    def send4(i):
        return pltpu.make_async_remote_copy(
            src_ref=g1_ref,
            dst_ref=recv4.at[me],
            send_sem=ssem4.at[i],
            recv_sem=rsem4.at[i],
            device_id={"unit": unit_at(i)},
            device_id_type=MESH,
        )

    @loop(1, n_unit)
    def _(i):
        send4(i).start()

    ring(1)
    ring(back)

    for q in range(side):
        for half in range(2):
            for way in (two,) if q in relayed else (1, back, two):
                origin = at_offset(half, q, way)

                @pl.when(whole(half, origin))
                def _():
                    for sub in (0, 1) if q in relayed else (None,):
                        arrived(half, origin, sub)

    recv4[me] = g1_ref[...]

    @loop(1, n_unit)
    def _(i):
        send4(i).wait_recv()

    total = recv4[0]
    for j in range(1, n_unit):
        total = total + recv4[j]
    step = total / (pltpu.roll(total, HALF, 1) + damping)
    nc_ref[...] = coef_ref[...] + step[:, :NCOEF]

    @loop(1, n_unit)
    def _(i):
        send1(i).wait_send()
        send4(i).wait_send()

    @loop(1, n_src)
    def _(i):
        send_coef(i).wait_send()
        send3(i).wait_send()
        other = row_at(i)
        by_group(other % groups, lambda rows: copy2(other, row, rows).wait_send())

    for half in range(2):
        for q in range(side):

            @pl.when(whole(half, at_offset(half, q, 0)))
            def _():
                for n in range(2 if q in relayed else 3):
                    pass_on(half, row, None, at_offset(half, 1, 0), (q, n)).wait_send()

            if q in relayed:
                for n in range(2):

                    @pl.when(whole(half, at_offset(half, q, (back, 1)[n])))
                    def _():
                        pass_on(half, row, n, at_offset(half, 1, 0), (q, 3 + n)).wait_send()

        @pl.when(whole(half, row))
        def _():
            for n in range(3):
                pass_on(half, row, None, at_offset(half, 1, 0), (side, n)).wait_send()


def widen_kernel(step, in_ref, nc_in, out_hbm, nc_hbm, wide_ref, sems):
    groups = in_ref.shape[0] // 2
    flat = wide_ref.shape[0]
    copies = [pltpu.make_async_copy(nc_in, nc_hbm, sems.at[groups])]
    copies[0].start()
    for group in range(groups):
        first, last = group * step, min((group + 1) * step, flat)
        for half in range(2):
            lanes = slice(half * LANES, (half + 1) * LANES)
            wide_ref[first:last, lanes] = in_ref[half * groups + group].astype(F32)[: last - first]
        rows = pl.ds(first, last - first)
        copies.append(pltpu.make_async_copy(wide_ref.at[rows], out_hbm.at[rows], sems.at[group]))
        copies[-1].start()
    for copy in copies:
        copy.wait()


def widen(gathered, new_coeffs, flat, step):
    vmem = pl.BlockSpec(memory_space=pltpu.VMEM)
    hbm = pl.BlockSpec(memory_space=pltpu.HBM)
    return pl.pallas_call(
        functools.partial(widen_kernel, step),
        out_shape=(
            jax.ShapeDtypeStruct((flat, 2 * LANES), F32),
            jax.ShapeDtypeStruct(new_coeffs.shape, F32),
        ),
        in_specs=[vmem, vmem],
        out_specs=(hbm, hbm),
        scratch_shapes=[
            pltpu.VMEM((flat, 2 * LANES), F32),
            pltpu.SemaphoreType.DMA((gathered.shape[0] // 2 + 1,)),
        ],
        compiler_params=pltpu.CompilerParams(vmem_limit_bytes=16 * 1024 * 1024),
    )(gathered, new_coeffs)


def body(coeffs, spectra, epoch_weight, source_blocks, epoch_owner, epoch_unit_local, design):
    n_src = lax.axis_size("src")
    n_unit = lax.axis_size("unit")
    epochs = spectra.shape[0]
    nblocks = epochs // BLOCK
    nsrc = coeffs.shape[0]
    units, flat = design.shape
    groups = n_src // 2
    samples = HALF // groups
    part_rows = samples * nsrc
    message = part_rows + up(nsrc, 16)
    all_src = n_src * nsrc
    side = math.isqrt(n_src)
    erows = up(samples * NCOEF, 64)
    vmem = pl.BlockSpec(memory_space=pltpu.VMEM)
    hbm = pl.BlockSpec(memory_space=pltpu.HBM)
    sems = pltpu.SemaphoreType.DMA
    gathered, new_coeffs = pl.pallas_call(
        functools.partial(kernel, n_src, n_unit, nsrc),
        out_shape=(
            jax.ShapeDtypeStruct((n_src, erows, LANES), BF),
            jax.ShapeDtypeStruct(coeffs.shape, F32),
        ),
        in_specs=[hbm] * 7,
        out_specs=(vmem, vmem),
        scratch_shapes=[
            pltpu.VMEM((NSAMP, epochs), BF),
            pltpu.VMEM((nblocks, BLOCK), BF),
            pltpu.VMEM((nblocks, BLOCK), jnp.int32),
            pltpu.VMEM((nblocks, BLOCK), jnp.int32),
            pltpu.VMEM((1, nsrc), jnp.int32),
            pltpu.VMEM(coeffs.shape, F32),
            pltpu.VMEM((flat, units), BF),
            pltpu.VMEM((n_unit * nblocks, LANES), F32),
            pltpu.VMEM((HALF, epochs), BF),
            pltpu.VMEM((SLOTS, epochs), BF),
            pltpu.VMEM((n_unit, HALF, SLOTS), BF),
            pltpu.VMEM((n_unit, HALF, SLOTS), BF),
            pltpu.VMEM((up(nsrc, 16), LANES), BF),
            pltpu.VMEM((n_src, up(nsrc, 16), LANES), BF),
            pltpu.VMEM((all_src, LANES), F32),
            pltpu.VMEM((samples * HALF, LANES), F32),
            pltpu.VMEM((n_unit * SLOTS, units), BF),
            pltpu.VMEM((up(nsrc, 16), n_unit * SLOTS), F32),
            pltpu.VMEM((HALF, n_unit * SLOTS), F32),
            pltpu.VMEM((part_rows, n_unit * SLOTS), BF),
            pltpu.VMEM((n_src, message, LANES), BF),
            pltpu.VMEM((n_src, message, LANES), BF),
            pltpu.VMEM((n_src * part_rows, LANES), F32),
            pltpu.VMEM((samples, all_src, LANES), F32),
            pltpu.VMEM((all_src, LANES), F32),
            pltpu.VMEM((samples, HALF, LANES), F32),
            pltpu.VMEM((erows, LANES), BF),
            pltpu.VMEM((all_src, LANES), F32),
            pltpu.VMEM((HALF, LANES), F32),
            pltpu.VMEM((n_src, nsrc, LANES), F32),
            pltpu.VMEM((nsrc, LANES), F32),
            pltpu.VMEM((n_unit, nsrc, LANES), F32),
            sems((7,)),
            sems((n_src,)),
            sems((n_src,)),
            sems((n_unit,)),
            sems((n_unit,)),
            sems((n_src,)),
            sems((n_src,)),
            sems((n_src,)),
            sems((n_src,)),
            sems((n_unit,)),
            sems((n_unit,)),
            sems((2, side + 1, 5)),
            sems((2, n_src, 2)),
            pltpu.SemaphoreType.REGULAR,
        ],
        compiler_params=pltpu.CompilerParams(
            collective_id=0, has_side_effects=True, vmem_limit_bytes=44 * 1024 * 1024
        ),
    )(
        *[
            pltpu.with_memory_space_constraint(x, pltpu.HBM)
            for x in (
                spectra.T,
                epoch_weight.reshape(nblocks, BLOCK),
                epoch_unit_local.reshape(nblocks, BLOCK),
                epoch_owner.reshape(nblocks, BLOCK),
                source_blocks,
                coeffs,
                design.T,
            )
        ]
    )
    new_design, new_coeffs = widen(gathered, new_coeffs, flat, samples * NCOEF)
    return (new_design.T, new_coeffs)


def solution(mesh):
    return jax.shard_map(
        body,
        mesh=mesh,
        in_specs=(
            P("src", None),
            P(("src", "unit"), None),
            P(("src", "unit")),
            P("src", None),
            P(("src", "unit"), None),
            P(("src", "unit")),
            P("unit", None),
        ),
        out_specs=(P("unit", None), P("src", None)),
        check_vma=False,
    )
```

```python
import functools
import math

import jax
import jax.numpy as jnp
from jax import lax
from jax.experimental import pallas as pl
from jax.experimental.pallas import tpu as pltpu
from jax.sharding import PartitionSpec as P

NCOEF = 55
NSAMP = 60
HALF = 64
LANES = 128
BLOCK = 128
SLOTS = 256
damping = 1.0

MESH = pl.DeviceIdType.MESH
BF = jnp.bfloat16
F32 = jnp.float32


def dot(a, b):
    return jnp.dot(a, b, preferred_element_type=F32)


def dot_nt(a, b):
    return lax.dot_general(a, b, (((1,), (1,)), ((), ())), preferred_element_type=F32)


def iota(shape, dim):
    return lax.broadcasted_iota(jnp.int32, shape, dim)


def ones_where(mask):
    return jnp.where(mask, 1.0, 0.0).astype(BF)


def split(x):
    high = x.astype(BF)
    return high, (x - high.astype(F32)).astype(BF)


def up(x, n):
    return -(-x // n) * n


def kernel(
    n_src,
    n_unit,
    nsrc,
    spec_hbm,
    w_hbm,
    u_hbm,
    o_hbm,
    cnt_hbm,
    coef_hbm,
    design_hbm,
    gbuf,
    nc_ref,
    spec_ref,
    w_ref,
    u_ref,
    o_ref,
    cnt_ref,
    coef_ref,
    dbuf,
    rank_ref,
    items_ref,
    place_ref,
    out1,
    recv1,
    cown,
    crecv,
    c_ref,
    dk_ref,
    table_ref,
    mark_ref,
    got_ref,
    xbuf,
    sbuf,
    recv2,
    sf_ref,
    ahead_ref,
    w2_ref,
    emap,
    eflat,
    gh_ref,
    csq_ref,
    recv3,
    g1_ref,
    recv4,
    lsem,
    csem,
    crsem,
    ssem1,
    rsem1,
    ssem2,
    rsem2,
    ssem3,
    rsem3,
    ssem4,
    rsem4,
    ssem5,
    rsem5,
    ready,
):
    row = lax.axis_index("src")
    me = lax.axis_index("unit")
    epochs = spec_ref.shape[1]
    nblocks = epochs // BLOCK
    units = 2 * LANES
    groups = n_src // 2
    samples = HALF // groups
    part_rows = samples * nsrc
    all_src = n_src * nsrc
    head = up(nsrc, 16)
    last_samples = NSAMP - (groups - 1) * samples
    side = math.isqrt(n_src)
    flat = dbuf.shape[0]
    owner_rows = samples * NCOEF
    half_rows = eflat.shape[0] // 2
    my_half, my_group = row // groups, row % groups

    def unit_at(i):
        return lax.rem(me + i, n_unit)

    def row_at(i):
        return lax.rem(row + i, n_src)

    def loop(lo, hi):
        return pl.loop(lo, hi)

    barrier = pltpu.get_barrier_semaphore()

    @loop(1, n_unit)
    def _(i):
        pl.semaphore_signal(barrier, inc=1, device_id={"unit": unit_at(i)}, device_id_type=MESH)

    px, py = row // side, row % side

    @loop(1, side)
    def _(i):
        across = lax.rem(px + i, side) * side + py
        along = px * side + lax.rem(py + i, side)
        pl.semaphore_signal(barrier, inc=1, device_id={"src": across}, device_id_type=MESH)
        pl.semaphore_signal(barrier, inc=1, device_id={"src": along}, device_id_type=MESH)

    loads = [
        pltpu.make_async_copy(a, b, lsem.at[n])
        for n, (a, b) in enumerate(
            [
                (o_hbm, o_ref),
                (cnt_hbm, cnt_ref),
                (w_hbm, w_ref),
                (u_hbm, u_ref),
                (spec_hbm, spec_ref),
                (coef_hbm, coef_ref),
                (design_hbm, dbuf),
            ]
        )
    ]
    for load in loads:
        load.start()
    for load in loads[:-1]:
        load.wait()

    owner = o_ref[...]
    marks = jnp.concatenate([jnp.where(owner == j, 1.0, 0.0) for j in range(n_unit)], axis=0)
    marks_lo = marks.astype(BF)
    earlier = ones_where(iota((LANES, LANES), 0) < iota((LANES, LANES), 1))
    inside = dot(marks_lo, earlier)
    totals = dot(marks_lo, jnp.ones((LANES, LANES), BF)).astype(BF)
    nrow = n_unit * nblocks
    a, b = iota((nrow, nrow), 0), iota((nrow, nrow), 1)
    before = ones_where((a // nblocks == b // nblocks) & (b < a))
    rank_ref[...] = jnp.where(marks > 0.0, inside + dot(before, totals), -1.0)

    count = jnp.broadcast_to(cnt_ref[...].astype(F32), (nblocks, nsrc)).astype(BF)
    upto = ones_where(iota((nsrc, LANES), 0) <= iota((nsrc, LANES), 1))
    cum = dot(count, upto)
    index = (me * nblocks + iota((nblocks, LANES), 0)).astype(F32)
    done = ones_where((cum <= index) & (iota((nblocks, LANES), 1) < nsrc))
    source = dot(done, jnp.ones((LANES, LANES), BF))
    weights, locals_ = w_ref[...].astype(F32), u_ref[...].astype(F32)

    def one_row(x):
        return jnp.concatenate([x[b : b + 1, :] for b in range(nblocks)], axis=1)

    spare = jnp.zeros((HALF - NSAMP - 3, epochs), F32)
    items_ref[0:48, :] = spec_ref[0:48, :]
    items_ref[48:64, :] = jnp.concatenate(
        [
            spec_ref[48:NSAMP, :].astype(F32),
            one_row(weights),
            one_row(locals_),
            one_row(source),
            spare,
        ],
        axis=0,
    ).astype(BF)

    coef_lo = coef_ref[...].astype(BF)
    widen = ones_where(iota((NCOEF, LANES), 0) == iota((NCOEF, LANES), 1))
    deepen = ones_where(iota((cown.shape[0], nsrc), 0) == iota((cown.shape[0], nsrc), 1))
    padded = dot(deepen, dot(coef_lo, widen).astype(BF)).astype(BF)
    cown[...] = padded
    crecv[row] = padded

    pl.semaphore_wait(barrier, n_unit - 1 + 2 * (side - 1))

    @loop(1, side)
    def _(i):
        along = px * side + lax.rem(py + i, side)
        pl.semaphore_signal(ready, inc=1, device_id={"src": along}, device_id_type=MESH)

    def send1(i):
        return pltpu.make_async_remote_copy(
            src_ref=out1.at[i],
            dst_ref=recv1.at[i],
            send_sem=ssem1.at[i],
            recv_sem=rsem1.at[i],
            device_id={"unit": unit_at(i)},
            device_id_type=MESH,
        )

    def send_coef(i):
        return pltpu.make_async_remote_copy(
            src_ref=cown,
            dst_ref=crecv.at[row],
            send_sem=csem.at[i],
            recv_sem=crsem.at[i],
            device_id={"src": row_at(i)},
            device_id_type=MESH,
        )

    def far_first(k):
        middle = n_unit // 2
        return lax.rem(middle + jnp.where(k % 2 == 1, (k + 1) // 2, n_unit - k // 2), n_unit)

    slot = iota((SLOTS, LANES), 0).astype(F32).astype(BF)
    one, zero = jnp.ones((), BF), jnp.zeros((), BF)

    @loop(0, n_unit)
    def _(k):
        i = far_first(k)
        ranks = rank_ref[pl.ds(pl.multiple_of(unit_at(i) * nblocks, nblocks), nblocks), :]
        for block in range(nblocks):
            line = jnp.broadcast_to(ranks[block : block + 1, :], (SLOTS, LANES)).astype(BF)
            place_ref[:, block * BLOCK : (block + 1) * BLOCK] = jnp.where(line == slot, one, zero)
        result = dot_nt(items_ref[...], place_ref[...]).astype(BF)
        out1[i] = result

        @pl.when(i > 0)
        def _():
            send1(i).start()

    pl.semaphore_wait(ready, side - 1)

    @loop(1, n_src)
    def _(i):
        send_coef(i).start()

    loads[-1].wait()
    window = up(owner_rows + 15, 16)
    first_row = my_group * owner_rows
    start = jnp.minimum(first_row // 16 * 16, (flat - window) // 16 * 16)
    tail = flat // 16 * 16
    lanes_half = pl.ds(pl.multiple_of(my_half * LANES, LANES), LANES)
    shape = (samples * HALF, window)
    want = iota(shape, 0) // HALF * NCOEF + iota(shape, 0) % HALF + first_row
    real = iota(shape, 0) % HALF < NCOEF
    pick = ones_where(real & (want == iota(shape, 1) + start))
    maps = dot(pick, dbuf[pl.ds(pl.multiple_of(start, 16), window), lanes_half])
    shape = (samples * HALF, flat - tail)
    want = iota(shape, 0) // HALF * NCOEF + iota(shape, 0) % HALF + first_row
    real = iota(shape, 0) % HALF < NCOEF
    late = iota(shape, 1) + tail
    pick = ones_where(real & (want == late) & (late >= start + window))
    dk_ref[...] = maps + dot(pick, dbuf[tail:flat, lanes_half])

    unit_row = iota((units, SLOTS), 0).astype(F32)
    source_row = iota((mark_ref.shape[0], SLOTS), 0).astype(F32)
    recv1[0] = out1[0]

    @loop(0, n_unit)
    def _(k):
        i = jnp.where(k == 0, 0, far_first(k - 1))

        @pl.when(i > 0)
        def _():
            send1(i).wait_recv()

        got = recv1[i].astype(F32)
        at = pl.ds(pl.multiple_of(i * SLOTS, SLOTS), SLOTS)
        wrow = jnp.broadcast_to(got[60:61], (units, SLOTS))
        urow = jnp.broadcast_to(got[61:62], (units, SLOTS))
        srow = got[62:63]
        table_ref[at, :] = jnp.where(unit_row == urow, wrow, 0.0).T.astype(BF)
        chosen = jnp.broadcast_to(srow, source_row.shape) == source_row
        mark_ref[:, at] = jnp.where(chosen, 1.0, 0.0)
        got_ref[:, at] = got

    weight_own = dot(mark_ref[...].astype(BF), table_ref[...]).astype(BF)

    def copy2(other, slot, rows):
        return pltpu.make_async_remote_copy(
            src_ref=sbuf.at[other, pl.ds(0, rows)],
            dst_ref=recv2.at[slot, pl.ds(0, rows)],
            send_sem=ssem2.at[other],
            recv_sem=rsem2.at[slot],
            device_id={"src": other},
            device_id_type=MESH,
        )

    def by_group(group, act):
        @pl.when(group < groups - 1)
        def _():
            act(head + part_rows)

        @pl.when(group == groups - 1)
        def _():
            act(head + last_samples * nsrc)

    @loop(0, groups)
    def _(k):
        if side == 4:
            turn = lax.rem(k, 4)
            dy = jnp.where(turn == 0, 2, jnp.where(turn == 1, 1, jnp.where(turn == 2, 3, 0)))
            dx = jnp.where(k < 4, jnp.where(k == 1, 0, 1), jnp.where(k == 5, 1, 0))
            group = lax.rem(my_group // side + dx, 2) * side + lax.rem(my_group + dy, side)
        else:
            group = lax.rem(my_group + 1 + k, groups)
        data = got_ref[pl.ds(pl.multiple_of(group * samples, 8), samples), :]
        chosen = mark_ref[0:nsrc, :]
        for m in range(0, samples, 2):
            both = [chosen * data[n : n + 1] for n in (m, m + 1)]
            xbuf[m * nsrc : (m + 2) * nsrc, :] = jnp.concatenate(both, axis=0).astype(BF)
        sums = dot(xbuf[...], table_ref[...]).astype(BF)
        for half in range(2):
            other = half * groups + group
            lanes = slice(half * LANES, (half + 1) * LANES)
            sbuf[other, 0:head, :] = weight_own[:, lanes]
            sbuf[other, head : head + part_rows, :] = sums[:, lanes]

            @pl.when(other != row)
            def _():
                by_group(group, lambda rows: copy2(other, row, rows).start())

    recv2[row] = sbuf[row]

    @loop(0, n_src)
    def _(i):
        @pl.when(i > 0)
        def _():
            send_coef(i).wait_recv()

    @loop(0, n_src)
    def _(r):
        at = pl.ds(pl.multiple_of(r * nsrc, 8), nsrc)
        c_ref[at, :] = crecv[r].astype(F32)[:nsrc]

    coef = c_ref[...]
    turned = coef.T[:HALF]
    turned_lo = turned.astype(BF)
    square_hi, square_lo = split(turned * turned)
    coef_all = coef[:, :HALF].astype(BF)
    for m in range(samples):
        ahead_ref[m] = dot(coef_all, dk_ref[m * HALF : (m + 1) * HALF, :].astype(BF))

    @loop(0, n_src)
    def _(i):
        r = row_at(i)

        @pl.when(i > 0)
        def _():
            by_group(my_group, lambda rows: copy2(r, r, rows).wait_recv())

        got = recv2[r].astype(F32)
        for m in range(samples):
            at = pl.ds(pl.multiple_of(m * all_src + r * nsrc, 8), nsrc)
            sf_ref[at, :] = got[head + m * nsrc : head + (m + 1) * nsrc]
        w2_ref[pl.ds(pl.multiple_of(r * nsrc, 8), nsrc), :] = got[:nsrc]

    weight_lo = w2_ref[...].astype(BF)
    diag = dot(square_hi, weight_lo) + dot(square_lo, weight_lo)
    scale = 1.0 / (diag + damping)

    def by_samples(act):
        for m in range(last_samples):
            act(m)

        @pl.when(my_group < groups - 1)
        def _():
            for m in range(last_samples, samples):
                act(m)

    def refine(m):
        base = dk_ref[m * HALF : (m + 1) * HALF, :]
        sums = sf_ref[m * all_src : (m + 1) * all_src, :]
        resid = (sums - w2_ref[...] * ahead_ref[m]).astype(BF)
        refined = (base + dot(turned_lo, resid) * scale).astype(BF).astype(F32)
        emap[m] = refined
        dk_ref[m * NCOEF : (m + 1) * NCOEF, :] = refined[:NCOEF]

    by_samples(refine)
    if owner_rows < eflat.shape[0]:
        dk_ref[owner_rows : eflat.shape[0], :] = jnp.zeros((eflat.shape[0] - owner_rows, LANES), F32)
    eflat[...] = dk_ref[0 : eflat.shape[0], :].astype(BF)

    part_piece = half_rows // 2

    def at_offset(half, first, second):
        dx, dy = (first, second) if half == 0 else (second, first)
        return lax.rem(px + dx, side) * side + lax.rem(py + dy, side)

    def pass_on(half, origin, sub, target, key):
        if sub is None:
            rows = pl.ds(half * half_rows, half_rows)
        else:
            rows = pl.ds(half * half_rows + sub * part_piece, part_piece)
        return pltpu.make_async_remote_copy(
            src_ref=gbuf.at[origin, rows],
            dst_ref=gbuf.at[origin, rows],
            send_sem=ssem5.at[half, key[0], key[1]],
            recv_sem=rsem5.at[half, origin, sub or 0],
            device_id={"src": target},
            device_id_type=MESH,
        )

    def whole(half, origin):
        if half == 0 or last_samples * NCOEF > half_rows:
            return origin >= 0
        return origin % groups != groups - 1

    back, two = side - 1, side // 2
    ways = (1, back)
    relayed = (0, 1, back)

    def send_block(half, q):
        for n, way in enumerate(ways if q in relayed else (1, two, back)):
            pass_on(half, at_offset(half, q, 0), None, at_offset(half, 0, way), (q, n)).start()

    def arrived(half, origin, sub):
        pass_on(half, origin, sub, at_offset(half, 1, 0), (0, 0)).wait_recv()

    def relay(half, q):
        for n, way in enumerate(ways):
            origin = at_offset(half, q, (back, 1)[n])

            @pl.when(whole(half, origin))
            def _():
                arrived(half, origin, None)
                pass_on(half, origin, n, at_offset(half, 0, way), (q, 3 + n)).start()

    gbuf[row] = eflat[...]
    for half in range(2):

        @pl.when(whole(half, row))
        def _():
            for n, way in enumerate((two, 1, back)):
                pass_on(half, row, None, at_offset(half, way, 0), (side, n)).start()

    for half in range(2):

        @pl.when(whole(half, row))
        def _():
            send_block(half, 0)

    gh_ref[...] = jnp.zeros_like(gh_ref)
    csq_ref[...] = jnp.zeros_like(csq_ref)
    blank = jnp.zeros((HALF, LANES), F32)

    def terms(m):
        refined = emap[m]
        sums = sf_ref[m * all_src : (m + 1) * all_src, :]
        resid = (sums - w2_ref[...] * dot(coef_all, refined.astype(BF))).astype(BF)
        gh_ref[...] += dot_nt(resid, jnp.concatenate([refined, blank], axis=0).astype(BF))
        csq_ref[...] += refined * refined

    by_samples(terms)
    curve_hi, curve_lo = split(jnp.concatenate([blank, csq_ref[...]], axis=0))
    weight_lo = w2_ref[...].astype(BF)
    gh_ref[...] += dot_nt(weight_lo, curve_hi) + dot_nt(weight_lo, curve_lo)

    def send3(i):
        return pltpu.make_async_remote_copy(
            src_ref=gh_ref.at[pl.ds(pl.multiple_of(row_at(i) * nsrc, 8), nsrc)],
            dst_ref=recv3.at[i],
            send_sem=ssem3.at[i],
            recv_sem=rsem3.at[i],
            device_id={"src": row_at(i)},
            device_id_type=MESH,
        )

    @loop(1, n_src)
    def _(i):
        send3(i).start()

    def forward(q):
        for half in range(2):
            origin = at_offset(half, q, 0)

            @pl.when(whole(half, origin))
            def _():
                arrived(half, origin, None)
                send_block(half, q)

    def ring(q):
        for half in range(2):
            relay(half, q)

    forward(1)
    forward(back)
    ring(0)
    forward(two)
    g1_ref[...] = gh_ref[pl.ds(pl.multiple_of(row * nsrc, 8), nsrc), :]

    @loop(1, n_src)
    def _(i):
        send3(i).wait_recv()
        g1_ref[...] += recv3[i]

    def send4(i):
        return pltpu.make_async_remote_copy(
            src_ref=g1_ref,
            dst_ref=recv4.at[me],
            send_sem=ssem4.at[i],
            recv_sem=rsem4.at[i],
            device_id={"unit": unit_at(i)},
            device_id_type=MESH,
        )

    @loop(1, n_unit)
    def _(i):
        send4(i).start()

    ring(1)
    ring(back)

    @loop(1, n_unit)
    def _(i):
        send1(i).wait_send()

    @loop(1, n_src)
    def _(i):
        send_coef(i).wait_send()
        send3(i).wait_send()
        other = row_at(i)
        by_group(other % groups, lambda rows: copy2(other, row, rows).wait_send())

    for half in range(2):

        @pl.when(whole(half, row))
        def _():
            for n in range(3):
                pass_on(half, row, None, at_offset(half, 1, 0), (side, n)).wait_send()

    for q in range(side):
        for half in range(2):
            for way in (two,) if q in relayed else (1, back, two):
                origin = at_offset(half, q, way)

                @pl.when(whole(half, origin))
                def _():
                    for sub in (0, 1) if q in relayed else (None,):
                        arrived(half, origin, sub)

    recv4[me] = g1_ref[...]

    @loop(1, n_unit)
    def _(i):
        send4(i).wait_recv()

    total = recv4[0]
    for j in range(1, n_unit):
        total = total + recv4[j]
    step = total / (pltpu.roll(total, HALF, 1) + damping)
    nc_ref[...] = coef_ref[...] + step[:, :NCOEF]

    @loop(1, n_unit)
    def _(i):
        send4(i).wait_send()

    for half in range(2):
        for q in range(side):

            @pl.when(whole(half, at_offset(half, q, 0)))
            def _():
                for n in range(2 if q in relayed else 3):
                    pass_on(half, row, None, at_offset(half, 1, 0), (q, n)).wait_send()

            if q in relayed:
                for n in range(2):

                    @pl.when(whole(half, at_offset(half, q, (back, 1)[n])))
                    def _():
                        pass_on(half, row, n, at_offset(half, 1, 0), (q, 3 + n)).wait_send()


def widen_kernel(step, in_ref, nc_in, out_hbm, nc_hbm, wide_ref, sems):
    groups = in_ref.shape[0] // 2
    flat = wide_ref.shape[0]
    copies = [pltpu.make_async_copy(nc_in, nc_hbm, sems.at[groups])]
    copies[0].start()
    for group in range(groups):
        first, last = group * step, min((group + 1) * step, flat)
        for half in range(2):
            lanes = slice(half * LANES, (half + 1) * LANES)
            wide_ref[first:last, lanes] = in_ref[half * groups + group].astype(F32)[: last - first]
        rows = pl.ds(first, last - first)
        copies.append(pltpu.make_async_copy(wide_ref.at[rows], out_hbm.at[rows], sems.at[group]))
        copies[-1].start()
    for copy in copies:
        copy.wait()


def widen(gathered, new_coeffs, flat, step):
    vmem = pl.BlockSpec(memory_space=pltpu.VMEM)
    hbm = pl.BlockSpec(memory_space=pltpu.HBM)
    return pl.pallas_call(
        functools.partial(widen_kernel, step),
        out_shape=(
            jax.ShapeDtypeStruct((flat, 2 * LANES), F32),
            jax.ShapeDtypeStruct(new_coeffs.shape, F32),
        ),
        in_specs=[vmem, vmem],
        out_specs=(hbm, hbm),
        scratch_shapes=[
            pltpu.VMEM((flat, 2 * LANES), F32),
            pltpu.SemaphoreType.DMA((gathered.shape[0] // 2 + 1,)),
        ],
        compiler_params=pltpu.CompilerParams(vmem_limit_bytes=16 * 1024 * 1024),
    )(gathered, new_coeffs)


def body(coeffs, spectra, epoch_weight, source_blocks, epoch_owner, epoch_unit_local, design):
    n_src = lax.axis_size("src")
    n_unit = lax.axis_size("unit")
    epochs = spectra.shape[0]
    nblocks = epochs // BLOCK
    nsrc = coeffs.shape[0]
    units, flat = design.shape
    groups = n_src // 2
    samples = HALF // groups
    part_rows = samples * nsrc
    message = part_rows + up(nsrc, 16)
    all_src = n_src * nsrc
    side = math.isqrt(n_src)
    erows = up(samples * NCOEF, 64)
    vmem = pl.BlockSpec(memory_space=pltpu.VMEM)
    hbm = pl.BlockSpec(memory_space=pltpu.HBM)
    sems = pltpu.SemaphoreType.DMA
    gathered, new_coeffs = pl.pallas_call(
        functools.partial(kernel, n_src, n_unit, nsrc),
        out_shape=(
            jax.ShapeDtypeStruct((n_src, erows, LANES), BF),
            jax.ShapeDtypeStruct(coeffs.shape, F32),
        ),
        in_specs=[hbm] * 7,
        out_specs=(vmem, vmem),
        scratch_shapes=[
            pltpu.VMEM((NSAMP, epochs), BF),
            pltpu.VMEM((nblocks, BLOCK), BF),
            pltpu.VMEM((nblocks, BLOCK), jnp.int32),
            pltpu.VMEM((nblocks, BLOCK), jnp.int32),
            pltpu.VMEM((1, nsrc), jnp.int32),
            pltpu.VMEM(coeffs.shape, F32),
            pltpu.VMEM((flat, units), BF),
            pltpu.VMEM((n_unit * nblocks, LANES), F32),
            pltpu.VMEM((HALF, epochs), BF),
            pltpu.VMEM((SLOTS, epochs), BF),
            pltpu.VMEM((n_unit, HALF, SLOTS), BF),
            pltpu.VMEM((n_unit, HALF, SLOTS), BF),
            pltpu.VMEM((up(nsrc, 16), LANES), BF),
            pltpu.VMEM((n_src, up(nsrc, 16), LANES), BF),
            pltpu.VMEM((all_src, LANES), F32),
            pltpu.VMEM((samples * HALF, LANES), F32),
            pltpu.VMEM((n_unit * SLOTS, units), BF),
            pltpu.VMEM((up(nsrc, 16), n_unit * SLOTS), F32),
            pltpu.VMEM((HALF, n_unit * SLOTS), F32),
            pltpu.VMEM((part_rows, n_unit * SLOTS), BF),
            pltpu.VMEM((n_src, message, LANES), BF),
            pltpu.VMEM((n_src, message, LANES), BF),
            pltpu.VMEM((n_src * part_rows, LANES), F32),
            pltpu.VMEM((samples, all_src, LANES), F32),
            pltpu.VMEM((all_src, LANES), F32),
            pltpu.VMEM((samples, HALF, LANES), F32),
            pltpu.VMEM((erows, LANES), BF),
            pltpu.VMEM((all_src, LANES), F32),
            pltpu.VMEM((HALF, LANES), F32),
            pltpu.VMEM((n_src, nsrc, LANES), F32),
            pltpu.VMEM((nsrc, LANES), F32),
            pltpu.VMEM((n_unit, nsrc, LANES), F32),
            sems((7,)),
            sems((n_src,)),
            sems((n_src,)),
            sems((n_unit,)),
            sems((n_unit,)),
            sems((n_src,)),
            sems((n_src,)),
            sems((n_src,)),
            sems((n_src,)),
            sems((n_unit,)),
            sems((n_unit,)),
            sems((2, side + 1, 5)),
            sems((2, n_src, 2)),
            pltpu.SemaphoreType.REGULAR,
        ],
        compiler_params=pltpu.CompilerParams(
            collective_id=0, has_side_effects=True, vmem_limit_bytes=44 * 1024 * 1024
        ),
    )(
        *[
            pltpu.with_memory_space_constraint(x, pltpu.HBM)
            for x in (
                spectra.T,
                epoch_weight.reshape(nblocks, BLOCK),
                epoch_unit_local.reshape(nblocks, BLOCK),
                epoch_owner.reshape(nblocks, BLOCK),
                source_blocks,
                coeffs,
                design.T,
            )
        ]
    )
    new_design, new_coeffs = widen(gathered, new_coeffs, flat, samples * NCOEF)
    return (new_design.T, new_coeffs)


def solution(mesh):
    return jax.shard_map(
        body,
        mesh=mesh,
        in_specs=(
            P("src", None),
            P(("src", "unit"), None),
            P(("src", "unit")),
            P("src", None),
            P(("src", "unit"), None),
            P(("src", "unit")),
            P("unit", None),
        ),
        out_specs=(P("unit", None), P("src", None)),
        check_vma=False,
    )
```
